512 devices in a mesh: ctx: 128 (over x_lo, y, z), ch: 4 (over x_hi, core).
Axes of the slice: x: 4 (x_hi: 2, x_lo: 2; x = x_hi * 2 + x_lo), y: 4, z: 16, core: 2. Of those that a mesh axis runs over, the one named last changes fastest.
Arguments:
- query_in: bfloat16 [16384, 4096], P('ctx', 'ch'), may hold values from -6 to 6
- key_in: bfloat16 [16384, 4096], P('ctx', 'ch'), may hold values from -6 to 6
- value_in: bfloat16 [16384, 4096], P('ctx', 'ch'), may hold values from -6 to 6
- short_filter: float32 [3, 3, 4096], P(None, None, 'ch'), may hold values from -3.5 to 3.5
- decay_rate: float32 [4096, 16], P('ch'), may hold values from 0.5 to 2000
- residue: float32 [4096, 16], P('ch'), may hold values from -1.5 to 1.5
- out_weight: bfloat16 [4096, 4096], P('ch', 'ctx'), may hold values from -0.09375 to 0.09375
Outputs:
- mixed: bfloat16 [16384, 4096], P(('ctx', 'ch'))
The draws below stay inside these ranges and needn't reach their ends.
All inputs are finite; a program needn't handle non-finite values.
Results may differ from the reference program's by a relative error of at most 0.0081.
Values may be sent and summed in bfloat16 or wider, within the bound.
A program may use at most 128 MiB of HBM per device.

```python
import math
import jax
import jax.numpy as jnp
from jax import lax

MODEL_DIM = 4096
CHANNELS = 4096
FILTER_MODES = 16
SHORT_TAPS = 3
TOKENS = 16384


def level_of(rng, shape, cuts, low, top_value):
    loudness = 1.0
    for axis_at, blocks in cuts:
        draws = jax.random.uniform(jax.random.fold_in(jax.random.fold_in(rng, 6), axis_at), (blocks,), jnp.float32, low / len(cuts), top_value / len(cuts))
        loudness = loudness * jnp.repeat(jnp.exp(draws), shape[axis_at] // blocks).reshape((-1,) + (1,) * (len(shape) - 1 - axis_at))
    return loudness


def noise(stream_key, shape, spread, most, shards=(), kind=jnp.bfloat16):
    gain = level_of(stream_key, shape, shards, -0.22, 0.18) if shards else 1.0
    entries = jax.random.normal(stream_key, shape, jnp.float32) * spread * gain
    return jnp.minimum(jnp.maximum(entries, -most), most).astype(kind)


def setup_inputs(seed: int = 0) -> dict:
    key_list = jax.random.split(jax.random.key(seed), 8)
    query_in = noise(key_list[0], (TOKENS, CHANNELS), 1.0, 6.0, ((0, 128), (1, 4)))
    key_in = noise(key_list[1], (TOKENS, CHANNELS), 1.0, 6.0, ((0, 128), (1, 4)))
    value_in = noise(key_list[2], (TOKENS, CHANNELS), 1.0, 6.0, ((0, 128), (1, 4)))
    short_filter = noise(key_list[3], (3, SHORT_TAPS, CHANNELS), SHORT_TAPS ** -0.5, 3.5, ((2, 4),), jnp.float32)
    decay_rate = jnp.clip(jnp.exp(math.log(2000.0) - 8.2940496 * jax.random.uniform(key_list[4], (CHANNELS, FILTER_MODES), jnp.float32) ** level_of(key_list[4], (CHANNELS, FILTER_MODES), ((0, 4),), -0.2, 0.2)), 0.5, 2000.0)
    residue = noise(key_list[5], (CHANNELS, FILTER_MODES), 0.25, 1.5, ((0, 4),), jnp.float32)
    out_weight = noise(key_list[6], (CHANNELS, MODEL_DIM), CHANNELS ** -0.5, 0.09375, ((0, 4), (1, 128)))
    return dict(query_in=query_in, key_in=key_in, value_in=value_in, short_filter=short_filter, decay_rate=decay_rate, residue=residue, out_weight=out_weight)


def modal_filter(decay_rate, residue, length_total, lag_count):
    decay = decay_rate / length_total
    weight = residue * jnp.sqrt(-jnp.expm1(-2.0 * decay))
    steps = jnp.arange(lag_count, dtype=jnp.float32)

    def add_mode(running, members):
        mode_decay, mode_weight = members
        return (running + mode_weight[:, None] * jnp.exp(-mode_decay[:, None] * steps[None, :]), None)
    start_value = jnp.zeros((decay_rate.shape[0], lag_count), jnp.float32)
    running, _ = lax.scan(add_mode, start_value, (decay.T, weight.T))
    return running

def short_conv(signal, taps):
    wide = signal.astype(jnp.float32)
    running = jnp.zeros(wide.shape, jnp.float32)
    for offset in range(SHORT_TAPS):
        moved = jnp.pad(wide, ((offset, 0), (0, 0)))[:wide.shape[0]]
        running = running + taps[offset][None, :] * moved
    return running.astype(jnp.bfloat16)

def reference(query_in, key_in, value_in, short_filter, decay_rate, residue, out_weight):
    query_conv = short_conv(query_in, short_filter[0])
    key_conv = short_conv(key_in, short_filter[1])
    value_conv = short_conv(value_in, short_filter[2])
    product = (key_conv.astype(jnp.float32) * value_conv.astype(jnp.float32)).astype(jnp.bfloat16)
    group_size = math.gcd(CHANNELS, 64)
    block_shape = (CHANNELS // group_size, group_size)
    product_rows = product.astype(jnp.float32).T.reshape(block_shape + (TOKENS,))
    rate_rows = decay_rate.reshape(block_shape + (FILTER_MODES,))
    residue_rows = residue.reshape(block_shape + (FILTER_MODES,))

    def one_block(members):
        signal, rate_block, residue_block = members
        filter_rows = modal_filter(rate_block, residue_block, TOKENS, TOKENS)
        spectrum = jnp.fft.rfft(signal, n=2 * TOKENS) * jnp.fft.rfft(filter_rows, n=2 * TOKENS)
        return jnp.fft.irfft(spectrum, n=2 * TOKENS)[:, :TOKENS]
    convolved = lax.map(one_block, (product_rows, rate_rows, residue_rows))
    long_part = convolved.reshape(CHANNELS, TOKENS).T.astype(jnp.bfloat16)
    gated = (query_conv.astype(jnp.float32) * long_part.astype(jnp.float32)).astype(jnp.bfloat16)
    return jnp.dot(gated, out_weight, preferred_element_type=jnp.float32).astype(jnp.bfloat16)
```

```python
import functools

import jax
import jax.numpy as jnp
from jax import lax
from jax.experimental import pallas as pl
from jax.experimental.pallas import tpu as pltpu
from jax.sharding import PartitionSpec as P

MESH = pl.DeviceIdType.MESH
F32 = jnp.float32
BF16 = jnp.bfloat16

XN, YN, ZN = 2, 4, 16
ROWS = XN * YN
TAPS = 3
MODES = 16
TOK = 128
CHN = 1024
TILES = CHN // 128
SEG = 8
STEPS = TOK // SEG
COLS = 32
RUN = ZN * COLS
QTR = TOK // 4


def rounded(x):
    return x.astype(BF16).astype(F32)


def kernel(
    q_ref, k_ref, v_ref, taps_ref, rate_ref, rate3_ref, weight_ref, wt_ref, out_ref,
    xs, halo_out, halo_in, prod, qconv, local, powers, ends, z_in, before, totals, carry_out, carry_in,
    gate, pooled, wg, part, part_out, part_in, half_out, half_in, done,
    halo_sem, z_sem, row_sem, back_sem, own_sem, other_sem, cross_sem, fore_sem, pool_sem, core_sem, hi_sem, out_sem,
):
    ctx = lax.axis_index("ctx")
    ch = lax.axis_index("ch")
    xl, y, z = ctx // (YN * ZN), (ctx // ZN) % YN, ctx % ZN
    row = ctx // ZN
    hi, core = ch // 2, ch % 2

    def at(xl, y, z):
        return ((xl * YN + y) * ZN + z, ch)

    def send(src, dst, sems, index, device):
        copy = pltpu.make_async_remote_copy(
            src_ref=src,
            dst_ref=dst,
            send_sem=sems.at[0, index],
            recv_sem=sems.at[1, index],
            device_id=device,
            device_id_type=MESH,
        )
        return copy

    nxt = ((ctx + 1) % (XN * YN * ZN), ch)
    prv = ((ctx + XN * YN * ZN - 1) % (XN * YN * ZN), ch)
    mate = (ctx, hi * 2 + 1 - core)
    far = (ctx, (1 - hi) * 2 + core)
    z_up, z_down = at(xl, y, (z + 1) % ZN), at(xl, y, (z + ZN - 1) % ZN)
    y_up, y_down = at(xl, (y + 1) % YN, z), at(xl, (y + YN - 1) % YN, z)
    y_far = at(xl, (y + 2) % YN, z)
    x_mate = at(1 - xl, y, z)

    barrier = pltpu.get_barrier_semaphore()

    def greet(device):
        pl.semaphore_signal(barrier, inc=1, device_id=device, device_id_type=MESH)

    for device in (nxt, prv, mate, far):
        greet(device)

    @pl.loop(1, ZN)
    def _(o):
        greet((row * ZN + (z + o) % ZN, ch))

    @pl.loop(1, ROWS)
    def _(o):
        greet((((row + o) % ROWS) * ZN + z, ch))

    streams = (q_ref, k_ref, v_ref)
    halo_out[...] = jnp.zeros_like(halo_out)
    for s, stream in enumerate(streams):
        halo_out[2 * s : 2 * s + 2, :] = stream[TOK - 16 :, :].astype(F32)[14:16]
    pl.semaphore_wait(barrier, 4 + (ZN - 1) + (ROWS - 1))

    started = []

    def go(copy):
        copy.start()
        started.append(copy)
        return copy

    halo = go(send(halo_out, halo_in, halo_sem, 0, nxt))

    wg[xl, z] = wt_ref[...]
    lower, upper = pl.ds(0, COLS // 2), pl.ds(COLS // 2, COLS // 2)

    def block(side, index, part_rows=None):
        ref = wg.at[side, lax.rem(index + 2 * ZN, ZN)]
        return ref if part_rows is None else ref.at[part_rows]

    HALF = ZN // 2
    own_up, own_down, other_up, other_down, fore = {}, {}, {}, {}, {}

    def start_own(step):
        if step < HALF:
            own_up[step] = go(send(block(xl, z - step), block(xl, z - step), own_sem, step, z_up))
        if step < HALF - 1:
            own_down[step] = go(
                send(block(xl, z + step), block(xl, z + step), own_sem, HALF + step, z_down)
            )

    def start_other(step):
        if step < HALF - 1:
            b = block(1 - xl, z - step, upper)
            other_up[step] = go(send(b, b, other_sem, step, z_up))
        if step < HALF:
            b = block(1 - xl, z + step, upper)
            other_down[step] = go(send(b, b, other_sem, HALF + step, z_down))

    def forward(name, index):
        b = block(xl, index, lower)
        fore[name] = go(send(b, b, fore_sem, name, x_mate))

    start_own(0)
    b = block(xl, z, upper)
    cross = go(send(b, b, cross_sem, 0, x_mate))
    forward(0, z)

    def tick(step):
        if step - 1 in own_up:
            own_up[step - 1].wait_recv()
        if step - 1 in own_down:
            own_down[step - 1].wait_recv()
        if step == 0:
            cross.wait_recv()
        else:
            start_own(step)
            if step - 1 in other_up:
                other_up[step - 1].wait_recv()
            if step - 1 in other_down:
                other_down[step - 1].wait_recv()
        start_other(step)
        if 1 <= step <= HALF:
            forward(step, z - step)
        if 1 <= step <= HALF - 1:
            forward(HALF + step, z + step)

    for s, stream in enumerate(streams):
        for j in range(TILES):
            xs[s, j, 8:, :] = stream[:, j * 128 : (j + 1) * 128].astype(F32)

    def convolved(s, j, i, x0, x1, x2):
        taps = taps_ref[j]
        f = [taps[s * TAPS + t : s * TAPS + t + 1] for t in range(TAPS)]
        return rounded((f[0] * x0 + f[1] * x1) + f[2] * x2)

    def features(j, first, last):
        prev = {}
        for s in range(3):
            prev[s] = [
                xs[s, j, pl.ds(8 + first - d, SEG, stride=STEPS), :] for d in (1, 2)
            ]
        for i in range(first, last):
            out = []
            for s in range(3):
                x0 = xs[s, j, pl.ds(8 + i, SEG, stride=STEPS), :]
                x1, x2 = prev[s]
                out.append(convolved(s, j, i, x0, x1, x2))
                prev[s] = [x0, x1]
            qconv[j, i] = out[0]
            prod[j, i] = rounded(out[1] * out[2])

    @pl.loop(0, TILES)
    def _(j):
        features(j, 2, STEPS)

    tick(0)

    halo.wait_recv()
    seen = jnp.where(ctx == 0, 0.0, 1.0).astype(F32)
    for s in range(3):
        for j in range(TILES):
            xs[s, j, 6:8, :] = halo_in[2 * s : 2 * s + 2, j * 128 : (j + 1) * 128] * seen

    segment = lax.broadcasted_iota(jnp.int32, (SEG, 128), 0)

    @pl.loop(0, TILES)
    def _(j):
        features(j, 0, 2)
        rate = rate_ref[j]
        keep = jnp.exp(-rate)
        decays = [jnp.broadcast_to(keep[n : n + 1], (SEG, 128)) for n in range(MODES)]
        states = [jnp.zeros((SEG, 128), F32) for _ in range(MODES)]
        for i in range(STEPS):
            p = prod[j, i]
            states = [d * st + p for d, st in zip(decays, states)]
        for n in range(MODES):
            a = rate[n : n + 1]
            total = states[n]
            for k in (1, 2, 4):
                moved = jnp.where(segment >= k, pltpu.roll(total, k, 0), 0.0)
                total = total + jnp.exp(a * (-float(STEPS * k))) * moved
            local[j, n] = jnp.where(segment >= 1, pltpu.roll(total, 1, 0), 0.0)
            powers[j, n] = jnp.exp(a * (segment * -STEPS).astype(F32))
            ends[n, pl.ds(j, 1), :] = total[SEG - 1 : SEG]

    def z_copy(o):
        to = (z + o) % ZN
        return send(ends.at[to], z_in.at[z], z_sem, o, (row * ZN + to, ch))

    @pl.loop(1, ZN)
    def _(o):
        z_copy(o).start()

    z_in[z] = ends[z]
    tick(1)

    @pl.loop(1, ZN)
    def _(o):
        z_copy(o).wait_recv()

    rate = rate3_ref[z]
    keep = jnp.exp(rate * -float(TOK))
    state = jnp.zeros((SEG, 128), F32)
    for zz in range(ZN):
        before[zz] = state
        state = keep * state + z_in[zz]
    totals[row] = state

    def row_copy(o):
        to = (row + o) % ROWS
        return send(totals.at[row], totals.at[row], row_sem, o, (to * ZN + z, ch))

    @pl.loop(1, ROWS)
    def _(o):
        row_copy(o).start()

    tick(2)

    @pl.loop(1, ROWS)
    def _(o):
        row_copy(o).wait_recv()

    keep_row = jnp.exp(rate * -float(TOK * ZN))
    state = jnp.zeros((SEG, 128), F32)
    for r in range(ROWS):
        state = jnp.where(r < row, keep_row * state + totals[r], state)
    for zz in range(ZN):
        carry_out[zz] = before[zz] + state
        state = keep * state

    def back_copy(o):
        to = (z + o) % ZN
        return send(carry_out.at[to], carry_in.at[z], back_sem, o, (row * ZN + to, ch))

    @pl.loop(1, ZN)
    def _(o):
        back_copy(o).start()

    carry_in[z] = carry_out[z]
    tick(3)

    @pl.loop(1, ZN)
    def _(o):
        back_copy(o).wait_recv()

    @pl.loop(0, TILES)
    def _(j):
        keep = jnp.exp(-rate_ref[j])
        weight = weight_ref[j]
        decays = [jnp.broadcast_to(keep[n : n + 1], (SEG, 128)) for n in range(MODES)]
        weights = [jnp.broadcast_to(weight[n : n + 1], (SEG, 128)) for n in range(MODES)]
        states = [
            local[j, n] + powers[j, n] * carry_in[n, pl.ds(j, 1), :] for n in range(MODES)
        ]
        for i in range(STEPS):
            p = prod[j, i]
            states = [d * st + p for d, st in zip(decays, states)]
            terms = [w * st for w, st in zip(weights, states)]
            while len(terms) > 1:
                terms = [a + b for a, b in zip(terms[::2], terms[1::2])]
            gate[j, pl.ds(i, SEG, stride=STEPS), :] = qconv[j, i] * rounded(terms[0])

    for j in range(TILES):
        pooled[0, :, j * 128 : (j + 1) * 128] = gate[j].astype(BF16)

    top, bottom = pl.ds(0, TOK // 2), pl.ds(TOK // 2, TOK // 2)

    def pool(slot, to_slot, rows, index, device):
        return go(send(pooled.at[slot, rows], pooled.at[to_slot, rows], pool_sem, index, device))

    up_a = pool(0, 1, top, 0, y_up)
    down_a = pool(0, 2, bottom, 1, y_down)
    up_b = pool(0, 1, bottom, 2, y_up)
    down_b = pool(0, 2, top, 3, y_down)

    for step in range(4, HALF + 1):
        tick(step)
    up_a.wait_recv()
    up_far = pool(1, 3, top, 4, y_up)
    down_a.wait_recv()
    down_far = pool(2, 3, bottom, 5, y_down)
    for copy in fore.values():
        copy.wait_recv()

    owners = (None, y_down, y_up, y_far)
    to_core, to_hi = {}, {}

    def project(b):
        for side in range(XN):
            sums = lax.dot_general(
                pooled[b],
                wg[side].reshape(RUN, CHN),
                (((1,), (1,)), ((), ())),
                preferred_element_type=F32,
            )
            for h in range(2):
                for c in range(2):
                    quarter = sums[(h * 2 + c) * QTR : (h * 2 + c + 1) * QTR]
                    part[b, c, h, side] = quarter
                    part_out[b, c, h, side] = quarter.astype(BF16)
        to_core[b] = go(send(part_out.at[b, 1 - core], part_in.at[b], core_sem, b, mate))

    def add_core(b):
        to_core[b].wait_recv()
        half_out[b] = (part[b, core, 1 - hi] + part_in[b, 1 - hi].astype(F32)).astype(BF16)
        to_hi[b] = go(send(half_out.at[b], half_in.at[b], hi_sem, b, far))

    def finish(b):
        to_hi[b].wait_recv()
        mixed = part[b, core, hi] + part_in[b, hi].astype(F32) + half_in[b].astype(F32)
        done[b] = mixed.astype(BF16)
        for side in range(XN):
            columns = pl.ds(pl.multiple_of(side * (YN * RUN) + y * RUN, RUN), RUN)
            if b == 0:
                out_ref[:, columns] = done[b, side]
            else:
                go(send(done.at[b, side], out_ref.at[:, columns], out_sem, b * XN + side, owners[b]))

    project(0)
    up_b.wait_recv()
    project(1)
    add_core(0)
    down_b.wait_recv()
    project(2)
    add_core(1)
    finish(0)
    up_far.wait_recv()
    down_far.wait_recv()
    project(3)
    add_core(2)
    finish(1)
    add_core(3)
    finish(2)
    finish(3)

    @pl.loop(1, ZN)
    def _(o):
        z_copy(o).wait_send()
        back_copy(o).wait_send()

    @pl.loop(1, ROWS)
    def _(o):
        row_copy(o).wait_send()

    for copy in started:
        copy.wait_send()

    for b, owner in ((1, y_up), (2, y_down), (3, y_far)):
        sender = (y + {1: 1, 2: YN - 1, 3: 2}[b]) % YN
        for side in range(XN):
            columns = pl.ds(pl.multiple_of(side * (YN * RUN) + sender * RUN, RUN), RUN)
            send(done.at[b, side], out_ref.at[:, columns], out_sem, b * XN + side, owner).wait_recv()


def shards(query_in, key_in, value_in, short_filter, decay_rate, residue, out_weight):
    tokens_total = TOK * XN * YN * ZN
    decay = decay_rate / tokens_total
    weight = residue * jnp.sqrt(-jnp.expm1(-2.0 * decay))
    rate = jnp.transpose(decay.reshape(TILES, 128, MODES), (0, 2, 1))
    rate3 = jnp.transpose(rate, (1, 0, 2))
    weight = jnp.transpose(weight.reshape(TILES, 128, MODES), (0, 2, 1))
    taps = jnp.transpose(short_filter.reshape(3 * TAPS, TILES, 128), (1, 0, 2))
    vmem = pl.BlockSpec(memory_space=pltpu.VMEM)

    def sems(count):
        return pltpu.SemaphoreType.DMA((2, count))

    half = ZN // 2
    return pl.pallas_call(
        kernel,
        out_shape=jax.ShapeDtypeStruct((QTR, 4096), BF16),
        in_specs=[vmem] * 8,
        out_specs=vmem,
        scratch_shapes=[
            pltpu.VMEM((3, TILES, 8 + TOK, 128), F32),
            pltpu.VMEM((8, CHN), F32),
            pltpu.VMEM((8, CHN), F32),
            pltpu.VMEM((TILES, STEPS, SEG, 128), F32),
            pltpu.VMEM((TILES, STEPS, SEG, 128), F32),
            pltpu.VMEM((TILES, MODES, SEG, 128), F32),
            pltpu.VMEM((TILES, MODES, SEG, 128), F32),
            pltpu.VMEM((MODES, TILES, 128), F32),
            pltpu.VMEM((ZN, TILES, 128), F32),
            pltpu.VMEM((ZN, TILES, 128), F32),
            pltpu.VMEM((ROWS, TILES, 128), F32),
            pltpu.VMEM((ZN, TILES, 128), F32),
            pltpu.VMEM((MODES, TILES, 128), F32),
            pltpu.VMEM((TILES, TOK, 128), F32),
            pltpu.VMEM((YN, TOK, CHN), BF16),
            pltpu.VMEM((XN, ZN, COLS, CHN), BF16),
            pltpu.VMEM((YN, 2, 2, XN, QTR, RUN), F32),
            pltpu.VMEM((YN, 2, 2, XN, QTR, RUN), BF16),
            pltpu.VMEM((YN, 2, XN, QTR, RUN), BF16),
            pltpu.VMEM((YN, XN, QTR, RUN), BF16),
            pltpu.VMEM((YN, XN, QTR, RUN), BF16),
            pltpu.VMEM((YN, XN, QTR, RUN), BF16),
            sems(1),
            sems(ZN),
            sems(ROWS),
            sems(ZN),
            sems(2 * half),
            sems(2 * half),
            sems(1),
            sems(ZN),
            sems(6),
            sems(YN),
            sems(YN),
            sems(YN * XN),
        ],
        compiler_params=pltpu.CompilerParams(
            collective_id=0, has_side_effects=True, vmem_limit_bytes=40 * 1024 * 1024
        ),
        cost_estimate=pl.CostEstimate(
            flops=2 * 4 * TOK * CHN * CHN, bytes_accessed=4 * 1024 * 1024, transcendentals=0
        ),
    )(query_in, key_in, value_in, taps, rate, rate3, weight, jnp.transpose(out_weight))


def solution(mesh):
    return jax.shard_map(
        shards,
        mesh=mesh,
        in_specs=(
            P("ctx", "ch"),
            P("ctx", "ch"),
            P("ctx", "ch"),
            P(None, None, "ch"),
            P("ch", None),
            P("ch", None),
            P("ch", "ctx"),
        ),
        out_specs=P(("ctx", "ch"), None),
        check_vma=False,
    )
```

```python
import jax
import jax.numpy as jnp
from jax import lax
from jax.experimental import pallas as pl
from jax.experimental.pallas import tpu as pltpu
from jax.sharding import PartitionSpec as P

MESH = pl.DeviceIdType.MESH
F32 = jnp.float32
BF16 = jnp.bfloat16

XN, YN, ZN = 2, 4, 16
ROWS = XN * YN
TAPS = 3
MODES = 16
TOK = 128
CHN = 1024
TILES = CHN // 128
SEG = 8
STEPS = TOK // SEG
COLS = 32
RUN = ZN * COLS
QTR = TOK // 4
HALF = ZN // 2
LENGTH = TOK * XN * YN * ZN


def rounded(x):
    return x.astype(BF16).astype(F32)


def mode_weight(rate, residue):
    square = rate * rate
    series = rate * (1.0 + square * (1.0 / 6.0 + square * (1.0 / 120.0 + square * (1.0 / 5040.0))))
    small = 2.0 * jnp.exp(-rate) * series
    large = 1.0 - jnp.exp(-2.0 * rate)
    return residue * jnp.sqrt(jnp.where(rate < 0.25, small, large))


def kernel(
    q_hbm, k_hbm, v_hbm, taps_hbm, rate_hbm, residue_hbm, wt_hbm, out_ref,
    q_in, k_in, v_in, taps_in, rate_in, residue_in, wt_in,
    taps, rates, keeps, weights, line_rate,
    xs, halo_out, halo_in, prod, qconv, local, powers, ends_own, ends, z_in, before, totals, carry_out, carry_in,
    gate, pooled, wg, part, part_out, part_in, last_out, last_in,
    load_sem, halo_sem, z_sem, row_sem, back_sem, ring_sem, cross_sem, fore_sem, pool_sem, core_sem, last_sem,
):
    ctx = lax.axis_index("ctx")
    ch = lax.axis_index("ch")
    xl, y, z = ctx // (YN * ZN), (ctx // ZN) % YN, ctx % ZN
    row = ctx // ZN
    hi, core = ch // 2, ch % 2

    loads = []
    for i, (src, dst) in enumerate(
        (
            (k_hbm, k_in), (v_hbm, v_in), (q_hbm, q_in), (wt_hbm, wt_in),
            (rate_hbm, rate_in), (taps_hbm, taps_in), (residue_hbm, residue_in),
        )
    ):
        loads.append(pltpu.make_async_copy(src, dst, load_sem.at[i]))
        loads[-1].start()

    def at(xl, y, z, ch=ch):
        return ((xl * YN + y) * ZN + z, ch)

    def send(src, dst, sems, index, device):
        return pltpu.make_async_remote_copy(
            src_ref=src,
            dst_ref=dst,
            send_sem=sems.at[0, index],
            recv_sem=sems.at[1, index],
            device_id=device,
            device_id_type=MESH,
        )

    nxt = ((ctx + 1) % (XN * YN * ZN), ch)
    prv = ((ctx + XN * YN * ZN - 1) % (XN * YN * ZN), ch)
    mate = (ctx, hi * 2 + 1 - core)
    far_ch = (1 - hi) * 2 + core
    z_up, z_down = at(xl, y, (z + 1) % ZN), at(xl, y, (z + ZN - 1) % ZN)
    y_of = (y, (y + YN - 1) % YN, (y + 1) % YN, (y + 2) % YN)
    y_down, y_up = at(xl, y_of[1], z), at(xl, y_of[2], z)
    x_mate = at(1 - xl, y, z)

    barrier = pltpu.get_barrier_semaphore()

    def greet(device):
        pl.semaphore_signal(barrier, inc=1, device_id=device, device_id_type=MESH)

    @pl.loop(1, ZN)
    def _(o):
        greet((row * ZN + (z + o) % ZN, ch))

    for device in (nxt, prv, mate):
        greet(device)
    for b in range(YN):
        greet(at(xl, y_of[b], z, far_ch))

    @pl.loop(1, ROWS)
    def _(o):
        greet((((row + o) % ROWS) * ZN + z, ch))

    halo_out[...] = jnp.zeros_like(halo_out)
    loads[0].wait()
    loads[1].wait()
    loads[2].wait()
    streams = (q_in, k_in, v_in)
    for s, stream in enumerate(streams):
        halo_out[2 * s : 2 * s + 2, :] = stream[TOK - 16 :, :].astype(F32)[14:16]
    loads[3].wait()
    wg[xl, z] = wt_in[...]
    pl.semaphore_wait(barrier, 3 + YN + (ZN - 1) + (ROWS - 1))

    started = []

    def go(copy):
        copy.start()
        started.append(copy)
        return copy

    halo = go(send(halo_out, halo_in, halo_sem, 0, nxt))

    lower, upper = pl.ds(0, COLS // 2), pl.ds(COLS // 2, COLS // 2)
    chunks = ((xl, upper), (xl, lower), (1 - xl, upper))
    ups, downs, fore = {}, {}, {}

    def piece(side, rows, index):
        return wg.at[side, lax.rem(index + 2 * ZN, ZN), rows]

    def pass_on(step, c):
        side, rows = chunks[c]
        if step < HALF - 1 or (step == HALF - 1 and c < 2):
            b = piece(side, rows, z - step)
            ups[step, c] = go(send(b, b, ring_sem, step * 3 + c, z_up))
        if step < HALF - 1 or (step == HALF - 1 and c == 2):
            b = piece(side, rows, z + step)
            downs[step, c] = go(send(b, b, ring_sem, (HALF + step) * 3 + c, z_down))

    def forward(name, index):
        b = piece(xl, lower, index)
        fore[name] = go(send(b, b, fore_sem, name, x_mate))

    b = piece(xl, upper, z)
    cross = go(send(b, b, cross_sem, 0, x_mate))
    pass_on(0, 0)
    pass_on(0, 1)
    forward(0, z)

    def tick(step):
        for c in range(3):
            if step == 0:
                if c == 2:
                    cross.wait_recv()
                    pass_on(0, 2)
                continue
            if (step - 1, c) in ups:
                ups[step - 1, c].wait_recv()
            if (step - 1, c) in downs:
                downs[step - 1, c].wait_recv()
            if step < HALF:
                pass_on(step, c)
            if c == 1:
                forward(step, z - step)
                if step < HALF:
                    forward(HALF + step, z + step)

    loads[4].wait()
    loads[5].wait()
    loads[6].wait()
    for j in range(TILES):
        lanes = slice(j * 128, (j + 1) * 128)
        rate = rate_in[:, lanes] * (1.0 / LENGTH)
        rates[j] = rate
        keeps[j] = jnp.exp(-rate)
        weights[j] = mode_weight(rate, residue_in[:, lanes])
        for s in range(3):
            for t in range(TAPS):
                taps[j, s * TAPS + t : s * TAPS + t + 1, :] = taps_in[s, t : t + 1, lanes]
        line_rate[j : j + 1, :] = rates[j, pl.ds(z, 1), :]
        for s, stream in enumerate(streams):
            xs[s, j, :8, :] = jnp.zeros((8, 128), F32)
            xs[s, j, 8:, :] = stream[:, lanes].astype(F32)

    def features(j, first, last):
        tap = taps[j]
        prev = [
            [xs[s, j, pl.ds(8 + first - d, SEG, stride=STEPS), :] for d in (1, 2)] for s in range(3)
        ]
        products = []
        for i in range(first, last):
            out = []
            for s in range(3):
                f = [tap[s * TAPS + t : s * TAPS + t + 1] for t in range(TAPS)]
                x0 = xs[s, j, pl.ds(8 + i, SEG, stride=STEPS), :]
                x1, x2 = prev[s]
                out.append(rounded((f[0] * x0 + f[1] * x1) + f[2] * x2))
                prev[s] = [x0, x1]
            qconv[j, i] = out[0]
            p = rounded(out[1] * out[2])
            prod[j, i] = p
            products.append(p)
        return products

    segment = lax.broadcasted_iota(jnp.int32, (SEG, 128), 0)
    later = segment >= 1

    @pl.loop(0, TILES)
    def _(j):
        features(j, 0, STEPS)

    tick(0)

    @pl.loop(0, TILES)
    def _(j):
        rate = rates[j]
        keep = keeps[j]
        decays = [jnp.broadcast_to(keep[n : n + 1], (SEG, 128)) for n in range(MODES)]
        states = [jnp.zeros((SEG, 128), F32) for _ in range(MODES)]
        for i in range(STEPS):
            p = prod[j, i]
            if i < TAPS - 1:
                p = jnp.where(later, p, 0.0)
            states = [d * st + p for d, st in zip(decays, states)]
        for n in range(MODES):
            a = rate[n : n + 1]
            total = states[n]
            for k in (1, 2, 4):
                moved = jnp.where(segment >= k, pltpu.roll(total, k, 0), 0.0)
                total = total + jnp.exp(a * (-float(STEPS * k))) * moved
            local[j, n] = jnp.where(later, pltpu.roll(total, 1, 0), 0.0)
            ends_own[j, n : n + 1, :] = total[SEG - 1 : SEG]

    halo.wait_recv()
    seen = jnp.where(ctx == 0, 0.0, 1.0).astype(F32)
    for s in range(3):
        for j in range(TILES):
            xs[s, j, 6:8, :] = halo_in[2 * s : 2 * s + 2, j * 128 : (j + 1) * 128] * seen

    def first_two(j):
        rate = rates[j]
        return prod[j, 0, 0:1] * jnp.exp(rate) + prod[j, 1, 0:1] * jnp.exp(2.0 * rate)

    @pl.loop(0, TILES)
    def _(j):
        features(j, 0, TAPS - 1)
        total = ends_own[j] + jnp.exp(rates[j] * -float(TOK)) * first_two(j)
        for n in range(MODES):
            ends[n, pl.ds(j, 1), :] = total[n : n + 1]

    def z_copy(o):
        to = (z + o) % ZN
        return send(ends.at[to], z_in.at[z], z_sem, o, (row * ZN + to, ch))

    @pl.loop(1, ZN)
    def _(o):
        z_copy(o).start()

    z_in[z] = ends[z]
    tick(1)

    @pl.loop(0, TILES)
    def _(j):
        rate = rates[j]
        extra = first_two(j)
        for n in range(MODES):
            power = jnp.exp(rate[n : n + 1] * (segment * -STEPS).astype(F32))
            powers[j, n] = power
            local[j, n] = local[j, n] + jnp.where(later, power * extra[n : n + 1], 0.0)

    tick(2)

    @pl.loop(1, ZN)
    def _(o):
        z_copy(o).wait_recv()

    rate = line_rate[...]
    keep = jnp.exp(rate * -float(TOK))
    state = jnp.zeros((SEG, 128), F32)
    for zz in range(ZN):
        before[zz] = state
        state = keep * state + z_in[zz]
    totals[row] = state

    def row_copy(o):
        to = (row + o) % ROWS
        return send(totals.at[row], totals.at[row], row_sem, o, (to * ZN + z, ch))

    @pl.loop(1, ROWS)
    def _(o):
        row_copy(o).start()

    tick(3)

    @pl.loop(1, ROWS)
    def _(o):
        row_copy(o).wait_recv()

    keep_row = jnp.exp(rate * -float(TOK * ZN))
    state = jnp.zeros((SEG, 128), F32)
    for r in range(ROWS):
        state = jnp.where(r < row, keep_row * state + totals[r], state)
    for zz in range(ZN):
        carry_out[zz] = before[zz] + state
        state = keep * state

    def back_copy(o):
        to = (z + o) % ZN
        return send(carry_out.at[to], carry_in.at[z], back_sem, o, (row * ZN + to, ch))

    @pl.loop(1, ZN)
    def _(o):
        back_copy(o).start()

    carry_in[z] = carry_out[z]
    tick(4)
    tick(5)

    @pl.loop(1, ZN)
    def _(o):
        back_copy(o).wait_recv()

    def gated(half):
        @pl.loop(half * (TILES // 2), (half + 1) * (TILES // 2))
        def _(j):
            keep = keeps[j]
            weight = weights[j]
            decays = [jnp.broadcast_to(keep[n : n + 1], (SEG, 128)) for n in range(MODES)]
            scales = [jnp.broadcast_to(weight[n : n + 1], (SEG, 128)) for n in range(MODES)]
            states = [
                local[j, n] + powers[j, n] * carry_in[n, pl.ds(j, 1), :] for n in range(MODES)
            ]
            for i in range(STEPS):
                p = prod[j, i]
                states = [d * st + p for d, st in zip(decays, states)]
                terms = [w * st for w, st in zip(scales, states)]
                while len(terms) > 1:
                    terms = [a + b for a, b in zip(terms[::2], terms[1::2])]
                gate[j, pl.ds(i, SEG, stride=STEPS), :] = qconv[j, i] * rounded(terms[0])

        for i in range(TILES // 2):
            lanes = slice(i * 128, (i + 1) * 128)
            pooled[0, half, :, lanes] = gate[half * (TILES // 2) + i].astype(BF16)

    def pool(slot, to_slot, half, index, device):
        return go(send(pooled.at[slot, half], pooled.at[to_slot, half], pool_sem, index, device))

    gated(0)
    up_a = pool(0, 1, 0, 0, y_up)
    gated(1)
    down_a = pool(0, 2, 1, 1, y_down)
    up_b = pool(0, 1, 1, 2, y_up)
    down_b = pool(0, 2, 0, 3, y_down)

    tick(6)
    tick(7)
    up_a.wait_recv()
    up_far = pool(1, 3, 0, 4, y_up)
    down_a.wait_recv()
    down_far = pool(2, 3, 1, 5, y_down)
    tick(8)
    for copy in fore.values():
        copy.wait_recv()

    to_core, to_owner = {}, {}

    def project(b):
        for side in range(XN):
            sums = 0.0
            for half in range(2):
                depth = slice(half * (CHN // 2), (half + 1) * (CHN // 2))
                sums = sums + lax.dot_general(
                    pooled[b, half],
                    wg[side, :, :, depth].reshape(RUN, CHN // 2),
                    (((1,), (1,)), ((), ())),
                    preferred_element_type=F32,
                )
            for h in range(2):
                for c in range(2):
                    quarter = sums[(h * 2 + c) * QTR : (h * 2 + c + 1) * QTR]
                    part[b, c, h, side] = quarter
                    part_out[b, c, h, side] = quarter.astype(BF16)
        to_core[b] = go(send(part_out.at[b, 1 - core], part_in.at[b], core_sem, b, mate))

    def add_core(b):
        to_core[b].wait_recv()
        for same, h in ((0, hi), (1, 1 - hi)):
            sums = part[b, core, h] + part_in[b, h].astype(F32)
            last_out[b, same] = sums.astype(BF16)
            if b == 0 and same == 0:
                last_in[0, 0] = sums.astype(BF16)
            else:
                to_owner[b, same] = go(
                    send(
                        last_out.at[b, same], last_in.at[b, same], last_sem, b * 2 + same,
                        at(xl, y_of[b], z, h * 2 + core),
                    )
                )

    def finish(b):
        for same in range(2):
            if (b, same) in to_owner:
                to_owner[b, same].wait_recv()
        mixed = last_in[b, 0].astype(F32) + last_in[b, 1].astype(F32)
        sender = (y + (0, 1, YN - 1, 2)[b]) % YN
        for side in range(XN):
            columns = pl.ds(pl.multiple_of(side * (YN * RUN) + sender * RUN, RUN), RUN)
            out_ref[:, columns] = mixed[side].astype(BF16)

    project(0)
    up_b.wait_recv()
    project(1)
    add_core(0)
    down_b.wait_recv()
    project(2)
    add_core(1)
    add_core(2)
    up_far.wait_recv()
    down_far.wait_recv()
    project(3)
    finish(0)
    add_core(3)
    finish(1)
    finish(2)
    finish(3)

    @pl.loop(1, ZN)
    def _(o):
        z_copy(o).wait_send()
        back_copy(o).wait_send()

    @pl.loop(1, ROWS)
    def _(o):
        row_copy(o).wait_send()

    for copy in started:
        copy.wait_send()


def shards(query_in, key_in, value_in, short_filter, decay_rate, residue, out_weight):
    def sems(count):
        return pltpu.SemaphoreType.DMA((2, count))

    return pl.pallas_call(
        kernel,
        out_shape=jax.ShapeDtypeStruct((QTR, 4096), BF16),
        in_specs=[pl.BlockSpec(memory_space=pl.ANY)] * 7,
        out_specs=pl.BlockSpec(memory_space=pltpu.VMEM),
        scratch_shapes=[
            pltpu.VMEM((TOK, CHN), BF16),
            pltpu.VMEM((TOK, CHN), BF16),
            pltpu.VMEM((TOK, CHN), BF16),
            pltpu.VMEM((3, TAPS, CHN), F32),
            pltpu.VMEM((MODES, CHN), F32),
            pltpu.VMEM((MODES, CHN), F32),
            pltpu.VMEM((COLS, CHN), BF16),
            pltpu.VMEM((TILES, 16, 128), F32),
            pltpu.VMEM((TILES, MODES, 128), F32),
            pltpu.VMEM((TILES, MODES, 128), F32),
            pltpu.VMEM((TILES, MODES, 128), F32),
            pltpu.VMEM((TILES, 128), F32),
            pltpu.VMEM((3, TILES, 8 + TOK, 128), F32),
            pltpu.VMEM((8, CHN), F32),
            pltpu.VMEM((8, CHN), F32),
            pltpu.VMEM((TILES, STEPS, SEG, 128), F32),
            pltpu.VMEM((TILES, STEPS, SEG, 128), F32),
            pltpu.VMEM((TILES, MODES, SEG, 128), F32),
            pltpu.VMEM((TILES, MODES, SEG, 128), F32),
            pltpu.VMEM((TILES, MODES, 128), F32),
            pltpu.VMEM((MODES, TILES, 128), F32),
            pltpu.VMEM((ZN, TILES, 128), F32),
            pltpu.VMEM((ZN, TILES, 128), F32),
            pltpu.VMEM((ROWS, TILES, 128), F32),
            pltpu.VMEM((ZN, TILES, 128), F32),
            pltpu.VMEM((MODES, TILES, 128), F32),
            pltpu.VMEM((TILES, TOK, 128), F32),
            pltpu.VMEM((YN, 2, TOK, CHN // 2), BF16),
            pltpu.VMEM((XN, ZN, COLS, CHN), BF16),
            pltpu.VMEM((YN, 2, 2, XN, QTR, RUN), F32),
            pltpu.VMEM((YN, 2, 2, XN, QTR, RUN), BF16),
            pltpu.VMEM((YN, 2, XN, QTR, RUN), BF16),
            pltpu.VMEM((YN, 2, XN, QTR, RUN), BF16),
            pltpu.VMEM((YN, 2, XN, QTR, RUN), BF16),
            pltpu.SemaphoreType.DMA((7,)),
            sems(1),
            sems(ZN),
            sems(ROWS),
            sems(ZN),
            sems(2 * HALF * 3),
            sems(1),
            sems(ZN),
            sems(6),
            sems(YN),
            sems(YN * 2),
        ],
        compiler_params=pltpu.CompilerParams(
            collective_id=0, has_side_effects=True, vmem_limit_bytes=56 * 1024 * 1024
        ),
        cost_estimate=pl.CostEstimate(
            flops=2 * 4 * TOK * CHN * CHN, bytes_accessed=4 * 1024 * 1024, transcendentals=0
        ),
    )(
        query_in, key_in, value_in, short_filter,
        jnp.transpose(decay_rate), jnp.transpose(residue), jnp.transpose(out_weight),
    )


def solution(mesh):
    return jax.shard_map(
        shards,
        mesh=mesh,
        in_specs=(
            P("ctx", "ch"),
            P("ctx", "ch"),
            P("ctx", "ch"),
            P(None, None, "ch"),
            P("ch", None),
            P("ch", None),
            P("ch", "ctx"),
        ),
        out_specs=P(("ctx", "ch"), None),
        check_vma=False,
    )
```

```python
import jax
import jax.numpy as jnp
from jax import lax
from jax.experimental import pallas as pl
from jax.experimental.pallas import tpu as pltpu
from jax.sharding import PartitionSpec as P

MESH = pl.DeviceIdType.MESH
F32 = jnp.float32
BF16 = jnp.bfloat16

XN, YN, ZN = 2, 4, 16
ROWS = XN * YN
TAPS = 3
MODES = 16
TOK = 128
CHN = 1024
TILES = CHN // 128
SEG = 8
STEPS = TOK // SEG
COLS = 32
RUN = ZN * COLS
QTR = TOK // 4
HALF = ZN // 2
NEAR = ZN // 4
LENGTH = TOK * XN * YN * ZN


def rounded(x):
    return x.astype(BF16).astype(F32)


def mode_weight(rate, residue):
    square = rate * rate
    series = rate * (1.0 + square * (1.0 / 6.0 + square * (1.0 / 120.0 + square * (1.0 / 5040.0))))
    small = 2.0 * jnp.exp(-rate) * series
    large = 1.0 - jnp.exp(-2.0 * rate)
    return residue * jnp.sqrt(jnp.where(rate < 0.25, small, large))


def kernel(
    q_hbm, k_hbm, v_hbm, taps_hbm, rate_hbm, residue_hbm, wt_hbm, out_ref,
    q_in, k_in, v_in, taps_in, rate_in, residue_in, wt_in,
    taps, rates, keeps, weights, line_rate,
    xs, halo_out, halo_in, prod, qconv, local, powers, ends_own, ends, z_in, before, totals, carry_out, carry_in,
    gate, pooled, wg, first, part, part_out, part_in, last_out, last_in,
    load_sem, line_sem, halo_sem, z_sem, row_sem, back_sem, ring_sem, fore_sem, pool_sem, core_sem, last_sem,
):
    ctx = lax.axis_index("ctx")
    ch = lax.axis_index("ch")
    xl, y, z = ctx // (YN * ZN), (ctx // ZN) % YN, ctx % ZN
    row = ctx // ZN
    hi, core = ch // 2, ch % 2

    loads = []
    for i, (src, dst) in enumerate(
        (
            (k_hbm, k_in), (v_hbm, v_in), (q_hbm, q_in), (wt_hbm, wt_in),
            (rate_hbm, rate_in), (taps_hbm, taps_in), (residue_hbm, residue_in),
        )
    ):
        loads.append(pltpu.make_async_copy(src, dst, load_sem.at[i]))
        loads[-1].start()

    def at(xl, y, z, ch=ch):
        return ((xl * YN + y) * ZN + z, ch)

    def send(src, dst, sems, index, device):
        return pltpu.make_async_remote_copy(
            src_ref=src,
            dst_ref=dst,
            send_sem=sems.at[0, index],
            recv_sem=sems.at[1, index],
            device_id=device,
            device_id_type=MESH,
        )

    nxt = ((ctx + 1) % (XN * YN * ZN), ch)
    prv = ((ctx + XN * YN * ZN - 1) % (XN * YN * ZN), ch)
    mate = (ctx, hi * 2 + 1 - core)
    far_ch = (1 - hi) * 2 + core
    z_up, z_down = at(xl, y, (z + 1) % ZN), at(xl, y, (z + ZN - 1) % ZN)
    y_of = (y, (y + YN - 1) % YN, (y + 1) % YN, (y + 2) % YN)
    y_down, y_up = at(xl, y_of[1], z), at(xl, y_of[2], z)
    x_mate = at(1 - xl, y, z)

    barrier = pltpu.get_barrier_semaphore()

    def greet(device):
        pl.semaphore_signal(barrier, inc=1, device_id=device, device_id_type=MESH)

    for o in range(1, NEAR + 1):
        greet(at(xl, y, (z + o) % ZN))
        greet(at(xl, y, (z + ZN - o) % ZN))
    for device in (nxt, prv, mate):
        greet(device)
    for b in range(YN):
        greet(at(xl, y_of[b], z, far_ch))

    @pl.loop(1, ROWS)
    def _(o):
        greet((((row + o) % ROWS) * ZN + z, ch))

    halo_out[...] = jnp.zeros_like(halo_out)
    loads[0].wait()
    loads[1].wait()
    loads[2].wait()
    streams = (q_in, k_in, v_in)
    for s, stream in enumerate(streams):
        halo_out[2 * s : 2 * s + 2, :] = stream[TOK - 16 :, :].astype(F32)[14:16]
    loads[3].wait()
    wg[xl, z] = wt_in[...]
    pl.semaphore_wait(barrier, 3 + YN + 2 * NEAR + (ROWS - 1))

    for o in (NEAR, ZN - NEAR):
        pl.semaphore_signal(line_sem, inc=1, device_id=at(xl, y, (z + o) % ZN), device_id_type=MESH)

    started = []

    def go(copy):
        copy.start()
        started.append(copy)
        return copy

    halo = go(send(halo_out, halo_in, halo_sem, 0, nxt))

    lower, upper = pl.ds(0, COLS // 2), pl.ds(COLS // 2, COLS // 2)
    ups, downs, fore = {}, {}, {}

    def block(index, rows=None):
        ref = wg.at[xl, lax.rem(index + 2 * ZN, ZN)]
        return ref if rows is None else ref.at[rows]

    def forward(name, index):
        fore[name] = go(send(block(index), block(index), fore_sem, name, x_mate))

    def pass_on(reach, c, hops):
        rows = (lower, upper)[c]
        if reach < HALF or c == 0:
            b = block(z - reach + hops, rows)
            ups[reach, c] = go(
                send(b, b, ring_sem, reach * 2 + c, at(xl, y, (z + hops) % ZN))
            )
        if reach < HALF or c == 1:
            b = block(z + reach - hops, rows)
            downs[reach, c] = go(
                send(b, b, ring_sem, (HALF + 1 + reach) * 2 + c, at(xl, y, (z + ZN - hops) % ZN))
            )

    for c in range(2):
        pass_on(2, c, 2)
    for c in range(2):
        pass_on(1, c, 1)
    forward(0, z)

    def arrived(reach, c):
        if (reach, c) in ups:
            ups[reach, c].wait_recv()
        if (reach, c) in downs:
            downs[reach, c].wait_recv()

    def tick(step):
        reach = step + 1
        for c in range(2):
            if reach == 2:
                arrived(1, c)
            arrived(reach, c)
            if reach < HALF:
                pass_on(reach + 1, c, 1)
        if reach == 2:
            forward(1, z - 1)
            forward(HALF + 1, z + 1)
        forward(reach, z - reach)
        if reach < HALF:
            forward(HALF + reach, z + reach)

    loads[4].wait()
    loads[5].wait()
    loads[6].wait()
    for j in range(TILES):
        lanes = slice(j * 128, (j + 1) * 128)
        rate = rate_in[:, lanes] * (1.0 / LENGTH)
        rates[j] = rate
        keeps[j] = jnp.exp(-rate)
        weights[j] = mode_weight(rate, residue_in[:, lanes])
        for s in range(3):
            for t in range(TAPS):
                taps[j, s * TAPS + t : s * TAPS + t + 1, :] = taps_in[s, t : t + 1, lanes]
        line_rate[j : j + 1, :] = rates[j, pl.ds(z, 1), :]
        for s, stream in enumerate(streams):
            xs[s, j, :8, :] = jnp.zeros((8, 128), F32)
            xs[s, j, 8:, :] = stream[:, lanes].astype(F32)

    def features(j, first, last):
        tap = taps[j]
        prev = [
            [xs[s, j, pl.ds(8 + first - d, SEG, stride=STEPS), :] for d in (1, 2)] for s in range(3)
        ]
        products = []
        for i in range(first, last):
            out = []
            for s in range(3):
                f = [tap[s * TAPS + t : s * TAPS + t + 1] for t in range(TAPS)]
                x0 = xs[s, j, pl.ds(8 + i, SEG, stride=STEPS), :]
                x1, x2 = prev[s]
                out.append(rounded((f[0] * x0 + f[1] * x1) + f[2] * x2))
                prev[s] = [x0, x1]
            qconv[j, i] = out[0]
            p = rounded(out[1] * out[2])
            prod[j, i] = p
            products.append(p)
        return products

    segment = lax.broadcasted_iota(jnp.int32, (SEG, 128), 0)
    later = segment >= 1

    @pl.loop(0, TILES)
    def _(j):
        features(j, 0, STEPS)

    @pl.loop(0, TILES)
    def _(j):
        rate = rates[j]
        keep = keeps[j]
        decays = [jnp.broadcast_to(keep[n : n + 1], (SEG, 128)) for n in range(MODES)]
        states = [jnp.zeros((SEG, 128), F32) for _ in range(MODES)]
        for i in range(STEPS):
            p = prod[j, i]
            if i < TAPS - 1:
                p = jnp.where(later, p, 0.0)
            states = [d * st + p for d, st in zip(decays, states)]
        for n in range(MODES):
            a = rate[n : n + 1]
            total = states[n]
            for k in (1, 2, 4):
                moved = jnp.where(segment >= k, pltpu.roll(total, k, 0), 0.0)
                total = total + jnp.exp(a * (-float(STEPS * k))) * moved
            local[j, n] = jnp.where(later, pltpu.roll(total, 1, 0), 0.0)
            ends_own[j, n : n + 1, :] = total[SEG - 1 : SEG]

    halo.wait_recv()
    seen = jnp.where(ctx == 0, 0.0, 1.0).astype(F32)
    for s in range(3):
        for j in range(TILES):
            xs[s, j, 6:8, :] = halo_in[2 * s : 2 * s + 2, j * 128 : (j + 1) * 128] * seen

    def first_two(j):
        rate = rates[j]
        return prod[j, 0, 0:1] * jnp.exp(rate) + prod[j, 1, 0:1] * jnp.exp(2.0 * rate)

    @pl.loop(0, TILES)
    def _(j):
        features(j, 0, TAPS - 1)
        total = ends_own[j] + jnp.exp(rates[j] * -float(TOK)) * first_two(j)
        for n in range(MODES):
            ends[n, pl.ds(j, 1), :] = total[n : n + 1]

    def z_copy(i):
        o = HALF + (i // 2) * (1 - 2 * (i % 2))
        to = (z + o) % ZN
        return send(ends.at[to], z_in.at[z], z_sem, o, (row * ZN + to, ch))

    pl.semaphore_wait(line_sem, 2)

    @pl.loop(1, ZN)
    def _(o):
        z_copy(o).start()

    z_in[z] = ends[z]
    tick(1)

    @pl.loop(0, TILES)
    def _(j):
        rate = rates[j]
        extra = first_two(j)
        for n in range(MODES):
            power = jnp.exp(rate[n : n + 1] * (segment * -STEPS).astype(F32))
            powers[j, n] = power
            local[j, n] = local[j, n] + jnp.where(later, power * extra[n : n + 1], 0.0)

    tick(2)

    @pl.loop(1, ZN)
    def _(o):
        z_copy(o).wait_recv()

    rate = line_rate[...]
    keep = jnp.exp(rate * -float(TOK))
    state = jnp.zeros((SEG, 128), F32)
    for zz in range(ZN):
        before[zz] = state
        state = keep * state + z_in[zz]
    totals[row] = state

    def row_copy(o):
        to = (row + o) % ROWS
        return send(totals.at[row], totals.at[row], row_sem, o, (to * ZN + z, ch))

    @pl.loop(1, ROWS)
    def _(o):
        row_copy(o).start()

    tick(3)
    tick(4)

    @pl.loop(1, ROWS)
    def _(o):
        row_copy(o).wait_recv()

    keep_row = jnp.exp(rate * -float(TOK * ZN))
    state = jnp.zeros((SEG, 128), F32)
    for r in range(ROWS):
        state = jnp.where(r < row, keep_row * state + totals[r], state)
    for zz in range(ZN):
        carry_out[zz] = before[zz] + state
        state = keep * state

    def back_copy(i):
        o = HALF + (i // 2) * (1 - 2 * (i % 2))
        to = (z + o) % ZN
        return send(carry_out.at[to], carry_in.at[z], back_sem, o, (row * ZN + to, ch))

    @pl.loop(1, ZN)
    def _(o):
        back_copy(o).start()

    carry_in[z] = carry_out[z]
    tick(5)
    tick(6)

    @pl.loop(1, ZN)
    def _(o):
        back_copy(o).wait_recv()

    def gated(half):
        @pl.loop(half * (TILES // 2), (half + 1) * (TILES // 2))
        def _(j):
            keep = keeps[j]
            weight = weights[j]
            decays = [jnp.broadcast_to(keep[n : n + 1], (SEG, 128)) for n in range(MODES)]
            scales = [jnp.broadcast_to(weight[n : n + 1], (SEG, 128)) for n in range(MODES)]
            states = [
                local[j, n] + powers[j, n] * carry_in[n, pl.ds(j, 1), :] for n in range(MODES)
            ]
            for i in range(STEPS):
                p = prod[j, i]
                states = [d * st + p for d, st in zip(decays, states)]
                terms = [w * st for w, st in zip(scales, states)]
                while len(terms) > 1:
                    terms = [a + b for a, b in zip(terms[::2], terms[1::2])]
                gate[j, pl.ds(i, SEG, stride=STEPS), :] = qconv[j, i] * rounded(terms[0])

        for i in range(TILES // 2):
            lanes = slice(i * 128, (i + 1) * 128)
            pooled[0, half, :, lanes] = gate[half * (TILES // 2) + i].astype(BF16)

    def pool(slot, to_slot, half, index, device):
        return go(send(pooled.at[slot, half], pooled.at[to_slot, half], pool_sem, index, device))

    gated(0)
    up_a = pool(0, 1, 0, 0, y_up)
    gated(1)
    down_a = pool(0, 2, 1, 1, y_down)
    up_b = pool(0, 1, 1, 2, y_up)
    down_b = pool(0, 2, 0, 3, y_down)

    tick(7)
    up_a.wait_recv()
    up_far = pool(1, 3, 0, 4, y_up)
    down_a.wait_recv()
    down_far = pool(2, 3, 1, 5, y_down)
    for copy in fore.values():
        copy.wait_recv()

    to_core, to_owner = {}, {}

    def product(b, half, side):
        depth = slice(half * (CHN // 2), (half + 1) * (CHN // 2))
        return lax.dot_general(
            pooled[b, half],
            wg[side, :, :, depth].reshape(RUN, CHN // 2),
            (((1,), (1,)), ((), ())),
            preferred_element_type=F32,
        )

    def project(b, sums):
        for side in range(XN):
            for h in range(2):
                for c in range(2):
                    quarter = sums[side][(h * 2 + c) * QTR : (h * 2 + c + 1) * QTR]
                    part[b, c, h, side] = quarter
                    part_out[b, c, h, side] = quarter.astype(BF16)
        to_core[b] = go(send(part_out.at[b, 1 - core], part_in.at[b], core_sem, b, mate))

    def both(b):
        return [product(b, 0, side) + product(b, 1, side) for side in range(XN)]

    def add_core(b):
        to_core[b].wait_recv()
        for same, h in ((0, hi), (1, 1 - hi)):
            sums = part[b, core, h] + part_in[b, h].astype(F32)
            last_out[b, same] = sums.astype(BF16)
            if b == 0 and same == 0:
                last_in[0, 0] = sums.astype(BF16)
            else:
                to_owner[b, same] = go(
                    send(
                        last_out.at[b, same], last_in.at[b, same], last_sem, b * 2 + same,
                        at(xl, y_of[b], z, h * 2 + core),
                    )
                )

    def finish(b):
        for same in range(2):
            if (b, same) in to_owner:
                to_owner[b, same].wait_recv()
        mixed = last_in[b, 0].astype(F32) + last_in[b, 1].astype(F32)
        sender = (y + (0, 1, YN - 1, 2)[b]) % YN
        for side in range(XN):
            columns = pl.ds(pl.multiple_of(side * (YN * RUN) + sender * RUN, RUN), RUN)
            out_ref[:, columns] = mixed[side].astype(BF16)

    project(0, both(0))
    up_b.wait_recv()
    project(1, both(1))
    add_core(0)
    down_b.wait_recv()
    project(2, both(2))
    add_core(1)
    up_far.wait_recv()
    for side in range(XN):
        first[side] = product(3, 0, side)
    add_core(2)
    down_far.wait_recv()
    project(3, [first[side] + product(3, 1, side) for side in range(XN)])
    finish(0)
    add_core(3)
    finish(1)
    finish(2)
    finish(3)

    @pl.loop(1, ZN)
    def _(o):
        z_copy(o).wait_send()
        back_copy(o).wait_send()

    @pl.loop(1, ROWS)
    def _(o):
        row_copy(o).wait_send()

    for copy in started:
        copy.wait_send()


def shards(query_in, key_in, value_in, short_filter, decay_rate, residue, out_weight):
    def sems(count):
        return pltpu.SemaphoreType.DMA((2, count))

    return pl.pallas_call(
        kernel,
        out_shape=jax.ShapeDtypeStruct((QTR, 4096), BF16),
        in_specs=[pl.BlockSpec(memory_space=pl.ANY)] * 7,
        out_specs=pl.BlockSpec(memory_space=pltpu.VMEM),
        scratch_shapes=[
            pltpu.VMEM((TOK, CHN), BF16),
            pltpu.VMEM((TOK, CHN), BF16),
            pltpu.VMEM((TOK, CHN), BF16),
            pltpu.VMEM((3, TAPS, CHN), F32),
            pltpu.VMEM((MODES, CHN), F32),
            pltpu.VMEM((MODES, CHN), F32),
            pltpu.VMEM((COLS, CHN), BF16),
            pltpu.VMEM((TILES, 16, 128), F32),
            pltpu.VMEM((TILES, MODES, 128), F32),
            pltpu.VMEM((TILES, MODES, 128), F32),
            pltpu.VMEM((TILES, MODES, 128), F32),
            pltpu.VMEM((TILES, 128), F32),
            pltpu.VMEM((3, TILES, 8 + TOK, 128), F32),
            pltpu.VMEM((8, CHN), F32),
            pltpu.VMEM((8, CHN), F32),
            pltpu.VMEM((TILES, STEPS, SEG, 128), F32),
            pltpu.VMEM((TILES, STEPS, SEG, 128), F32),
            pltpu.VMEM((TILES, MODES, SEG, 128), F32),
            pltpu.VMEM((TILES, MODES, SEG, 128), F32),
            pltpu.VMEM((TILES, MODES, 128), F32),
            pltpu.VMEM((MODES, TILES, 128), F32),
            pltpu.VMEM((ZN, TILES, 128), F32),
            pltpu.VMEM((ZN, TILES, 128), F32),
            pltpu.VMEM((ROWS, TILES, 128), F32),
            pltpu.VMEM((ZN, TILES, 128), F32),
            pltpu.VMEM((MODES, TILES, 128), F32),
            pltpu.VMEM((TILES, TOK, 128), F32),
            pltpu.VMEM((YN, 2, TOK, CHN // 2), BF16),
            pltpu.VMEM((XN, ZN, COLS, CHN), BF16),
            pltpu.VMEM((XN, TOK, RUN), F32),
            pltpu.VMEM((YN, 2, 2, XN, QTR, RUN), F32),
            pltpu.VMEM((YN, 2, 2, XN, QTR, RUN), BF16),
            pltpu.VMEM((YN, 2, XN, QTR, RUN), BF16),
            pltpu.VMEM((YN, 2, XN, QTR, RUN), BF16),
            pltpu.VMEM((YN, 2, XN, QTR, RUN), BF16),
            pltpu.SemaphoreType.DMA((7,)),
            pltpu.SemaphoreType.REGULAR,
            sems(1),
            sems(ZN),
            sems(ROWS),
            sems(ZN),
            sems(2 * (HALF + 1) * 2),
            sems(ZN),
            sems(6),
            sems(YN),
            sems(YN * 2),
        ],
        compiler_params=pltpu.CompilerParams(
            collective_id=0, has_side_effects=True, vmem_limit_bytes=56 * 1024 * 1024
        ),
        cost_estimate=pl.CostEstimate(
            flops=2 * 4 * TOK * CHN * CHN, bytes_accessed=4 * 1024 * 1024, transcendentals=0
        ),
    )(
        query_in, key_in, value_in, short_filter,
        jnp.transpose(decay_rate), jnp.transpose(residue), jnp.transpose(out_weight),
    )


def solution(mesh):
    return jax.shard_map(
        shards,
        mesh=mesh,
        in_specs=(
            P("ctx", "ch"),
            P("ctx", "ch"),
            P("ctx", "ch"),
            P(None, None, "ch"),
            P("ch", None),
            P("ch", None),
            P("ch", "ctx"),
        ),
        out_specs=P(("ctx", "ch"), None),
        check_vma=False,
    )
```

```python
import jax
import jax.numpy as jnp
from jax import lax
from jax.experimental import pallas as pl
from jax.experimental.pallas import tpu as pltpu
from jax.sharding import PartitionSpec as P

MESH = pl.DeviceIdType.MESH
F32 = jnp.float32
BF16 = jnp.bfloat16

XN, YN, ZN = 2, 4, 16
ROWS = XN * YN
TAPS = 3
MODES = 16
TOK = 128
CHN = 1024
TILES = CHN // 128
SEG = 8
STEPS = TOK // SEG
COLS = 32
RUN = ZN * COLS
SPAN = RUN // 2
QTR = TOK // 4
HALF = ZN // 2
RING = ZN // 2
REACH = RING // 2
NEAR = ZN // 4
LENGTH = TOK * XN * YN * ZN


def rounded(x):
    return x.astype(BF16).astype(F32)


def mode_weight(rate, residue):
    square = rate * rate
    series = rate * (1.0 + square * (1.0 / 6.0 + square * (1.0 / 120.0 + square * (1.0 / 5040.0))))
    small = 2.0 * jnp.exp(-rate) * series
    large = 1.0 - jnp.exp(-2.0 * rate)
    return residue * jnp.sqrt(jnp.where(rate < 0.25, small, large))


def kernel(
    q_hbm, k_hbm, v_hbm, taps_hbm, rate_hbm, residue_hbm, wt_hbm, out_ref,
    q_in, k_in, v_in, taps_in, rate_in, residue_in, wt_in,
    taps, rates, keeps, weights, line_rate,
    xs, halo_out, halo_in, prod, qconv, local, powers, ends_own, ends, z_in, before, totals, carry_out, carry_in,
    gate, pooled, wg, first, part, part_out, part_in, last_out, last_in, woven, turns,
    load_sem, line_sem, halo_sem, z_sem, row_sem, back_sem, ring_sem, twin_sem, fore_sem, pool_sem, core_sem, last_sem,
):
    ctx = lax.axis_index("ctx")
    ch = lax.axis_index("ch")
    xl, y, z = ctx // (YN * ZN), (ctx // ZN) % YN, ctx % ZN
    row = ctx // ZN
    hi, core = ch // 2, ch % 2

    loads = []
    for i, (src, dst) in enumerate(
        (
            (k_hbm, k_in), (v_hbm, v_in), (q_hbm, q_in), (wt_hbm, wt_in),
            (rate_hbm, rate_in), (taps_hbm, taps_in), (residue_hbm, residue_in),
        )
    ):
        loads.append(pltpu.make_async_copy(src, dst, load_sem.at[i]))
        loads[-1].start()

    def at(xl, y, z, ch=ch):
        return ((xl * YN + y) * ZN + z, ch)

    def send(src, dst, sems, index, device):
        return pltpu.make_async_remote_copy(
            src_ref=src,
            dst_ref=dst,
            send_sem=sems.at[0, index],
            recv_sem=sems.at[1, index],
            device_id=device,
            device_id_type=MESH,
        )

    nxt = ((ctx + 1) % (XN * YN * ZN), ch)
    prv = ((ctx + XN * YN * ZN - 1) % (XN * YN * ZN), ch)
    mate = (ctx, hi * 2 + 1 - core)
    far_ch = (1 - hi) * 2 + core
    x_mate = at(1 - xl, y, z)

    y_of = (y, y + 1 - 2 * (y % 2), y, y + 1 - 2 * (y % 2))
    z_of = (z, z, z + 1 - 2 * (z % 2), z + 1 - 2 * (z % 2))
    y_mate, z_mate = at(xl, y_of[1], z), at(xl, y, z_of[2])
    y_twin = at(xl, YN - 1 - y, z)

    barrier = pltpu.get_barrier_semaphore()

    def greet(device):
        pl.semaphore_signal(barrier, inc=1, device_id=device, device_id_type=MESH)

    for o in range(1, NEAR + 1):
        greet(at(xl, y, (z + o) % ZN))
        greet(at(xl, y, (z + ZN - o) % ZN))
    for device in (nxt, prv, mate):
        greet(device)
    for b in range(4):
        greet(at(xl, y_of[b], z_of[b], far_ch))
    greet(at(xl, y_of[3], z_of[3]))

    @pl.loop(1, ROWS)
    def _(o):
        greet((((row + o) % ROWS) * ZN + z, ch))

    halo_out[...] = jnp.zeros_like(halo_out)
    loads[0].wait()
    loads[1].wait()
    loads[2].wait()
    streams = (q_in, k_in, v_in)
    for s, stream in enumerate(streams):
        halo_out[2 * s : 2 * s + 2, :] = stream[TOK - 16 :, :].astype(F32)[14:16]
    loads[3].wait()
    wg[xl * 2 + y // 2, z // 2] = wt_in[...]
    pl.semaphore_wait(barrier, 3 + 5 + 2 * NEAR + (ROWS - 1))

    for o in (NEAR, ZN - NEAR):
        pl.semaphore_signal(line_sem, inc=1, device_id=at(xl, y, (z + o) % ZN), device_id_type=MESH)

    started = []

    def go(copy):
        copy.start()
        started.append(copy)
        return copy

    halo = go(send(halo_out, halo_in, halo_sem, 0, nxt))

    lower, upper = pl.ds(0, COLS // 2), pl.ds(COLS // 2, COLS // 2)
    ups, downs, twin, fore = {}, {}, {}, {}
    place = xl * 2 + y // 2
    beside = xl * 2 + 1 - y // 2

    def block(where, index, rows=None):
        ref = wg.at[where, lax.rem(index + 2 * RING, RING)]
        return ref if rows is None else ref.at[rows]

    def forward(name, index):
        b = block(place, index)
        twin[name] = go(send(b, b, twin_sem, name, y_twin))
        fore[name] = go(send(b, b, fore_sem, name, x_mate))

    def forward_beside(name, index):
        twin[name].wait_recv()
        b = block(beside, index)
        fore[RING + name] = go(send(b, b, fore_sem, RING + name, x_mate))

    def pass_on(reach, c):
        rows = (lower, upper)[c]
        if reach < REACH or c == 0:
            b = block(place, z // 2 - reach + 1, rows)
            ups[reach, c] = go(send(b, b, ring_sem, reach * 2 + c, at(xl, y, (z + 2) % ZN)))
        if reach < REACH or c == 1:
            b = block(place, z // 2 + reach - 1, rows)
            downs[reach, c] = go(
                send(b, b, ring_sem, (REACH + 1 + reach) * 2 + c, at(xl, y, (z + ZN - 2) % ZN))
            )

    for c in range(2):
        pass_on(1, c)
    forward(0, z // 2)

    def names(reach):
        if reach == 0:
            return [(0, 0)]
        return [(reach, -reach)] + ([(REACH + reach, reach)] if reach < REACH else [])

    def tick(reach):
        for c in range(2):
            if (reach, c) in ups:
                ups[reach, c].wait_recv()
            if (reach, c) in downs:
                downs[reach, c].wait_recv()
            if reach < REACH:
                pass_on(reach + 1, c)
        if reach <= REACH:
            for name, away in names(reach):
                forward(name, z // 2 + away)
        for name, away in names(reach - 1):
            forward_beside(name, z // 2 + away)

    source = lax.broadcasted_iota(jnp.int32, (RUN, RUN), 0)
    target = lax.broadcasted_iota(jnp.int32, (RUN, RUN), 1)
    parity = (source // SPAN + z) % 2
    wanted = (source % SPAN) // COLS * (2 * COLS) + parity * COLS + source % COLS
    turns[...] = jnp.where(wanted == target, 1.0, 0.0).astype(BF16)

    loads[4].wait()
    loads[5].wait()
    loads[6].wait()
    for j in range(TILES):
        lanes = slice(j * 128, (j + 1) * 128)
        rate = rate_in[:, lanes] * (1.0 / LENGTH)
        rates[j] = rate
        keeps[j] = jnp.exp(-rate)
        weights[j] = mode_weight(rate, residue_in[:, lanes])
        for s in range(3):
            for t in range(TAPS):
                taps[j, s * TAPS + t : s * TAPS + t + 1, :] = taps_in[s, t : t + 1, lanes]
        line_rate[j : j + 1, :] = rates[j, pl.ds(z, 1), :]
        for s, stream in enumerate(streams):
            xs[s, j, :8, :] = jnp.zeros((8, 128), F32)
            xs[s, j, 8:, :] = stream[:, lanes].astype(F32)

    def features(j, first, last):
        tap = taps[j]
        prev = [
            [xs[s, j, pl.ds(8 + first - d, SEG, stride=STEPS), :] for d in (1, 2)] for s in range(3)
        ]
        products = []
        for i in range(first, last):
            out = []
            for s in range(3):
                f = [tap[s * TAPS + t : s * TAPS + t + 1] for t in range(TAPS)]
                x0 = xs[s, j, pl.ds(8 + i, SEG, stride=STEPS), :]
                x1, x2 = prev[s]
                out.append(rounded((f[0] * x0 + f[1] * x1) + f[2] * x2))
                prev[s] = [x0, x1]
            qconv[j, i] = out[0]
            p = rounded(out[1] * out[2])
            prod[j, i] = p
            products.append(p)
        return products

    segment = lax.broadcasted_iota(jnp.int32, (SEG, 128), 0)
    later = segment >= 1

    @pl.loop(0, TILES)
    def _(j):
        features(j, 0, STEPS)

    @pl.loop(0, TILES)
    def _(j):
        rate = rates[j]
        keep = keeps[j]
        decays = [jnp.broadcast_to(keep[n : n + 1], (SEG, 128)) for n in range(MODES)]
        states = [jnp.zeros((SEG, 128), F32) for _ in range(MODES)]
        for i in range(STEPS):
            p = prod[j, i]
            if i < TAPS - 1:
                p = jnp.where(later, p, 0.0)
            states = [d * st + p for d, st in zip(decays, states)]
        for n in range(MODES):
            a = rate[n : n + 1]
            total = states[n]
            for k in (1, 2, 4):
                moved = jnp.where(segment >= k, pltpu.roll(total, k, 0), 0.0)
                total = total + jnp.exp(a * (-float(STEPS * k))) * moved
            local[j, n] = jnp.where(later, pltpu.roll(total, 1, 0), 0.0)
            ends_own[j, n : n + 1, :] = total[SEG - 1 : SEG]

    halo.wait_recv()
    seen = jnp.where(ctx == 0, 0.0, 1.0).astype(F32)
    for s in range(3):
        for j in range(TILES):
            xs[s, j, 6:8, :] = halo_in[2 * s : 2 * s + 2, j * 128 : (j + 1) * 128] * seen

    def first_two(j):
        rate = rates[j]
        return prod[j, 0, 0:1] * jnp.exp(rate) + prod[j, 1, 0:1] * jnp.exp(2.0 * rate)

    @pl.loop(0, TILES)
    def _(j):
        features(j, 0, TAPS - 1)
        total = ends_own[j] + jnp.exp(rates[j] * -float(TOK)) * first_two(j)
        for n in range(MODES):
            ends[n, pl.ds(j, 1), :] = total[n : n + 1]

    def z_copy(i):
        o = HALF + (i // 2) * (1 - 2 * (i % 2))
        to = (z + o) % ZN
        return send(ends.at[to], z_in.at[z], z_sem, o, (row * ZN + to, ch))

    pl.semaphore_wait(line_sem, 2)

    @pl.loop(1, ZN)
    def _(o):
        z_copy(o).start()

    z_in[z] = ends[z]

    @pl.loop(0, TILES)
    def _(j):
        rate = rates[j]
        extra = first_two(j)
        for n in range(MODES):
            power = jnp.exp(rate[n : n + 1] * (segment * -STEPS).astype(F32))
            powers[j, n] = power
            local[j, n] = local[j, n] + jnp.where(later, power * extra[n : n + 1], 0.0)

    tick(1)

    @pl.loop(1, ZN)
    def _(o):
        z_copy(o).wait_recv()


    rate = line_rate[...]
    keep = jnp.exp(rate * -float(TOK))
    state = jnp.zeros((SEG, 128), F32)
    for zz in range(ZN):
        before[zz] = state
        state = keep * state + z_in[zz]
    totals[row] = state

    def row_copy(o):
        to = (row + o) % ROWS
        return send(totals.at[row], totals.at[row], row_sem, o, (to * ZN + z, ch))

    @pl.loop(1, ROWS)
    def _(o):
        row_copy(o).start()


    tick(2)

    @pl.loop(1, ROWS)
    def _(o):
        row_copy(o).wait_recv()


    keep_row = jnp.exp(rate * -float(TOK * ZN))
    state = jnp.zeros((SEG, 128), F32)
    for r in range(ROWS):
        state = jnp.where(r < row, keep_row * state + totals[r], state)
    for zz in range(ZN):
        carry_out[zz] = before[zz] + state
        state = keep * state

    def back_copy(i):
        o = HALF + (i // 2) * (1 - 2 * (i % 2))
        to = (z + o) % ZN
        return send(carry_out.at[to], carry_in.at[z], back_sem, o, (row * ZN + to, ch))

    @pl.loop(1, ZN)
    def _(o):
        back_copy(o).start()

    carry_in[z] = carry_out[z]

    tick(3)
    tick(4)

    @pl.loop(1, ZN)
    def _(o):
        back_copy(o).wait_recv()


    def gated(half):
        @pl.loop(half * (TILES // 2), (half + 1) * (TILES // 2))
        def _(j):
            keep = keeps[j]
            weight = weights[j]
            decays = [jnp.broadcast_to(keep[n : n + 1], (SEG, 128)) for n in range(MODES)]
            scales = [jnp.broadcast_to(weight[n : n + 1], (SEG, 128)) for n in range(MODES)]
            states = [
                local[j, n] + powers[j, n] * carry_in[n, pl.ds(j, 1), :] for n in range(MODES)
            ]
            for i in range(STEPS):
                p = prod[j, i]
                states = [d * st + p for d, st in zip(decays, states)]
                terms = [w * st for w, st in zip(scales, states)]
                while len(terms) > 1:
                    terms = [a + b for a, b in zip(terms[::2], terms[1::2])]
                gate[j, pl.ds(i, SEG, stride=STEPS), :] = qconv[j, i] * rounded(terms[0])

        for i in range(TILES // 2):
            lanes = slice(i * 128, (i + 1) * 128)
            pooled[half, 0, :, lanes] = gate[half * (TILES // 2) + i].astype(BF16)

    def pool(slot, to_slot, half, index, device):
        return go(send(pooled.at[half, slot], pooled.at[half, to_slot], pool_sem, index, device))

    gated(0)
    z_a = pool(0, 2, 0, 0, z_mate)
    gated(1)
    y_a = pool(0, 1, 1, 1, y_mate)
    z_b = pool(0, 2, 1, 2, z_mate)
    y_b = pool(0, 1, 0, 3, y_mate)

    tick(5)

    to_core, to_owner = {}, {}

    def product(first_b, last_b, half, side):
        depth = slice(half * (CHN // 2), (half + 1) * (CHN // 2))
        return lax.dot_general(
            pooled[half, first_b : last_b + 1].reshape((last_b + 1 - first_b) * TOK, CHN // 2),
            wg[2 * side : 2 * side + 2, :, :, depth].reshape(RUN, CHN // 2),
            (((1,), (1,)), ((), ())),
            preferred_element_type=F32,
        )

    def project(b, side, sums):
        for h in range(2):
            for c in range(2):
                quarter = sums[(h * 2 + c) * QTR : (h * 2 + c + 1) * QTR]
                part[b, c, h, side] = quarter
                part_out[b, c, h, side] = quarter.astype(BF16)

    def whole(first_b, last_b):
        for side in range(XN):
            sums = product(first_b, last_b, 0, side) + product(first_b, last_b, 1, side)
            for b in range(first_b, last_b + 1):
                project(b, side, sums[(b - first_b) * TOK : (b + 1 - first_b) * TOK])
        for b in range(first_b, last_b + 1):
            exchange(b)

    def exchange(b):
        to_core[b] = go(send(part_out.at[b, 1 - core], part_in.at[b], core_sem, b, mate))

    def add_core(b):
        to_core[b].wait_recv()
        for same, h in ((1, 1 - hi), (0, hi)):
            sums = part[b, core, h] + part_in[b, h].astype(F32)
            last_out[b, same] = sums.astype(BF16)
            if b == 0 and same == 0:
                last_in[0, 0] = sums.astype(BF16)
            else:
                to_owner[b, same] = go(
                    send(
                        last_out.at[b, same], last_in.at[b, same], last_sem, b * 2 + same,
                        at(xl, y_of[b], z_of[b], h * 2 + core),
                    )
                )

    def finish(bs):
        for i, b in enumerate(bs):
            for same in range(2):
                if (b, same) in to_owner:
                    to_owner[b, same].wait_recv()
            mixed = (last_in[b, 0].astype(F32) + last_in[b, 1].astype(F32)).astype(BF16)
            for side in range(XN):
                for k in range(2):
                    woven[side * 2 + k, :, i * SPAN : (i + 1) * SPAN] = mixed[side, :, k * SPAN : (k + 1) * SPAN]
        spread = lax.dot_general(
            woven[...].reshape(4 * QTR, RUN), turns[...], (((1,), (0,)), ((), ())),
            preferred_element_type=F32,
        ).astype(BF16)
        sender = y_of[bs[0]]
        role = (sender + sender // 2) % 2
        for side in range(XN):
            for k, at_y in enumerate((role, YN - 1 - role)):
                columns = pl.ds(pl.multiple_of(side * (YN * RUN) + at_y * RUN, RUN), RUN)
                out_ref[:, columns] = spread[(side * 2 + k) * QTR : (side * 2 + k + 1) * QTR]

    z_a.wait_recv()
    far_a = pool(2, 3, 0, 4, y_mate)
    y_a.wait_recv()
    far_b = pool(1, 3, 1, 5, z_mate)
    for copy in fore.values():
        copy.wait_recv()
    whole(0, 0)
    y_b.wait_recv()
    z_b.wait_recv()
    whole(1, 2)
    add_core(0)
    far_a.wait_recv()
    for side in range(XN):
        first[side] = product(3, 3, 0, side)
    add_core(1)
    add_core(2)
    far_b.wait_recv()
    for side in range(XN):
        project(3, side, first[side] + product(3, 3, 1, side))
    exchange(3)
    finish((0, 2))
    add_core(3)
    finish((1, 3))

    @pl.loop(1, ZN)
    def _(o):
        z_copy(o).wait_send()
        back_copy(o).wait_send()

    @pl.loop(1, ROWS)
    def _(o):
        row_copy(o).wait_send()

    for copy in started:
        copy.wait_send()


def shards(query_in, key_in, value_in, short_filter, decay_rate, residue, out_weight):
    def sems(count):
        return pltpu.SemaphoreType.DMA((2, count))

    return pl.pallas_call(
        kernel,
        out_shape=jax.ShapeDtypeStruct((QTR, 4096), BF16),
        in_specs=[pl.BlockSpec(memory_space=pl.ANY)] * 7,
        out_specs=pl.BlockSpec(memory_space=pltpu.VMEM),
        scratch_shapes=[
            pltpu.VMEM((TOK, CHN), BF16),
            pltpu.VMEM((TOK, CHN), BF16),
            pltpu.VMEM((TOK, CHN), BF16),
            pltpu.VMEM((3, TAPS, CHN), F32),
            pltpu.VMEM((MODES, CHN), F32),
            pltpu.VMEM((MODES, CHN), F32),
            pltpu.VMEM((COLS, CHN), BF16),
            pltpu.VMEM((TILES, 16, 128), F32),
            pltpu.VMEM((TILES, MODES, 128), F32),
            pltpu.VMEM((TILES, MODES, 128), F32),
            pltpu.VMEM((TILES, MODES, 128), F32),
            pltpu.VMEM((TILES, 128), F32),
            pltpu.VMEM((3, TILES, 8 + TOK, 128), F32),
            pltpu.VMEM((8, CHN), F32),
            pltpu.VMEM((8, CHN), F32),
            pltpu.VMEM((TILES, STEPS, SEG, 128), F32),
            pltpu.VMEM((TILES, STEPS, SEG, 128), F32),
            pltpu.VMEM((TILES, MODES, SEG, 128), F32),
            pltpu.VMEM((TILES, MODES, SEG, 128), F32),
            pltpu.VMEM((TILES, MODES, 128), F32),
            pltpu.VMEM((MODES, TILES, 128), F32),
            pltpu.VMEM((ZN, TILES, 128), F32),
            pltpu.VMEM((ZN, TILES, 128), F32),
            pltpu.VMEM((ROWS, TILES, 128), F32),
            pltpu.VMEM((ZN, TILES, 128), F32),
            pltpu.VMEM((MODES, TILES, 128), F32),
            pltpu.VMEM((TILES, TOK, 128), F32),
            pltpu.VMEM((2, 4, TOK, CHN // 2), BF16),
            pltpu.VMEM((2 * XN, RING, COLS, CHN), BF16),
            pltpu.VMEM((XN, TOK, RUN), F32),
            pltpu.VMEM((YN, 2, 2, XN, QTR, RUN), F32),
            pltpu.VMEM((YN, 2, 2, XN, QTR, RUN), BF16),
            pltpu.VMEM((YN, 2, XN, QTR, RUN), BF16),
            pltpu.VMEM((YN, 2, XN, QTR, RUN), BF16),
            pltpu.VMEM((YN, 2, XN, QTR, RUN), BF16),
            pltpu.VMEM((4, QTR, RUN), BF16),
            pltpu.VMEM((RUN, RUN), BF16),
            pltpu.SemaphoreType.DMA((7,)),
            pltpu.SemaphoreType.REGULAR,
            sems(1),
            sems(ZN),
            sems(ROWS),
            sems(ZN),
            sems(2 * (REACH + 1) * 2),
            sems(RING),
            sems(ZN),
            sems(6),
            sems(YN),
            sems(YN * 2),
        ],
        compiler_params=pltpu.CompilerParams(
            collective_id=0, has_side_effects=True, vmem_limit_bytes=56 * 1024 * 1024
        ),
        cost_estimate=pl.CostEstimate(
            flops=2 * 4 * TOK * CHN * CHN, bytes_accessed=4 * 1024 * 1024, transcendentals=0
        ),
    )(
        query_in, key_in, value_in, short_filter,
        jnp.transpose(decay_rate), jnp.transpose(residue), jnp.transpose(out_weight),
    )


def solution(mesh):
    return jax.shard_map(
        shards,
        mesh=mesh,
        in_specs=(
            P("ctx", "ch"),
            P("ctx", "ch"),
            P("ctx", "ch"),
            P(None, None, "ch"),
            P("ch", None),
            P("ch", None),
            P("ch", "ctx"),
        ),
        out_specs=P(("ctx", "ch"), None),
        check_vma=False,
    )
```

```python
import jax
import jax.numpy as jnp
from jax import lax
from jax.experimental import pallas as pl
from jax.experimental.pallas import tpu as pltpu
from jax.sharding import PartitionSpec as P

MESH = pl.DeviceIdType.MESH
F32 = jnp.float32
BF16 = jnp.bfloat16

XN, YN, ZN = 2, 4, 16
ROWS = XN * YN
TAPS = 3
MODES = 16
TOK = 128
CHN = 1024
TILES = CHN // 128
SEG = 8
STEPS = TOK // SEG
COLS = 32
RUN = ZN * COLS
SPAN = RUN // 2
QTR = TOK // 4
HALF = ZN // 2
RING = ZN // 2
REACH = RING // 2
NEAR = ZN // 4
LENGTH = TOK * XN * YN * ZN


def rounded(x):
    return x.astype(BF16).astype(F32)


def mode_weight(rate, residue):
    square = rate * rate
    series = rate * (1.0 + square * (1.0 / 6.0 + square * (1.0 / 120.0 + square * (1.0 / 5040.0))))
    small = 2.0 * jnp.exp(-rate) * series
    large = 1.0 - jnp.exp(-2.0 * rate)
    return residue * jnp.sqrt(jnp.where(rate < 0.25, small, large))


def kernel(
    q_hbm, k_hbm, v_hbm, taps_hbm, rate_hbm, residue_hbm, wt_hbm, out_ref,
    q_in, k_in, v_in, taps_in, rate_in, residue_in, wt_in,
    taps, rates, keeps, weights, line_rate,
    xs, halo_out, halo_in, prod, qconv, local, powers, ends_own, ends, z_in, before, totals, carry_out, carry_in,
    gate, pooled, wg, first, part, part_out, part_in, last_out, last_in, woven, turns,
    load_sem, line_sem, halo_sem, z_sem, row_sem, back_sem, ring_sem, twin_sem, fore_sem, pool_sem, core_sem, last_sem,
):
    ctx = lax.axis_index("ctx")
    ch = lax.axis_index("ch")
    xl, y, z = ctx // (YN * ZN), (ctx // ZN) % YN, ctx % ZN
    row = ctx // ZN
    hi, core = ch // 2, ch % 2

    loads = []
    for i, (src, dst) in enumerate(
        (
            (k_hbm, k_in), (v_hbm, v_in), (q_hbm, q_in), (wt_hbm, wt_in),
            (rate_hbm, rate_in), (taps_hbm, taps_in), (residue_hbm, residue_in),
        )
    ):
        loads.append(pltpu.make_async_copy(src, dst, load_sem.at[i]))
        loads[-1].start()

    def at(xl, y, z, ch=ch):
        return ((xl * YN + y) * ZN + z, ch)

    def send(src, dst, sems, index, device):
        return pltpu.make_async_remote_copy(
            src_ref=src,
            dst_ref=dst,
            send_sem=sems.at[0, index],
            recv_sem=sems.at[1, index],
            device_id=device,
            device_id_type=MESH,
        )

    nxt = ((ctx + 1) % (XN * YN * ZN), ch)
    prv = ((ctx + XN * YN * ZN - 1) % (XN * YN * ZN), ch)
    mate = (ctx, hi * 2 + 1 - core)
    far_ch = (1 - hi) * 2 + core
    x_mate = at(1 - xl, y, z)

    y_of = (y, y + 1 - 2 * (y % 2), y, y + 1 - 2 * (y % 2))
    z_of = (z, z, z + 1 - 2 * (z % 2), z + 1 - 2 * (z % 2))
    y_mate, z_mate = at(xl, y_of[1], z), at(xl, y, z_of[2])
    y_twin = at(xl, YN - 1 - y, z)

    barrier = pltpu.get_barrier_semaphore()

    def greet(device):
        pl.semaphore_signal(barrier, inc=1, device_id=device, device_id_type=MESH)

    for o in range(1, NEAR + 1):
        greet(at(xl, y, (z + o) % ZN))
        greet(at(xl, y, (z + ZN - o) % ZN))
    for device in (nxt, prv, mate):
        greet(device)
    for b in range(4):
        greet(at(xl, y_of[b], z_of[b], far_ch))
    greet(at(xl, y_of[3], z_of[3]))

    @pl.loop(1, ROWS)
    def _(o):
        greet((((row + o) % ROWS) * ZN + z, ch))

    halo_out[...] = jnp.zeros_like(halo_out)
    loads[0].wait()
    loads[1].wait()
    loads[2].wait()
    streams = (q_in, k_in, v_in)
    for s, stream in enumerate(streams):
        halo_out[2 * s : 2 * s + 2, :] = stream[TOK - 16 :, :].astype(F32)[14:16]
    loads[3].wait()
    wg[xl * 2 + y // 2, z // 2] = wt_in[...]
    pl.semaphore_wait(barrier, 3 + 5 + 2 * NEAR + (ROWS - 1))

    for o in (NEAR, ZN - NEAR):
        pl.semaphore_signal(line_sem, inc=1, device_id=at(xl, y, (z + o) % ZN), device_id_type=MESH)

    started = []

    def go(copy):
        copy.start()
        started.append(copy)
        return copy

    halo = go(send(halo_out, halo_in, halo_sem, 0, nxt))

    lower, upper = pl.ds(0, COLS // 2), pl.ds(COLS // 2, COLS // 2)
    ups, downs, twin, fore = {}, {}, {}, {}
    place = xl * 2 + y // 2
    beside = xl * 2 + 1 - y // 2

    def block(where, index, rows=None):
        ref = wg.at[where, lax.rem(index + 2 * RING, RING)]
        return ref if rows is None else ref.at[rows]

    def forward(name, index):
        b = block(place, index)
        twin[name] = go(send(b, b, twin_sem, name, y_twin))
        fore[name] = go(send(b, b, fore_sem, name, x_mate))

    def forward_beside(name, index):
        twin[name].wait_recv()
        b = block(beside, index)
        fore[RING + name] = go(send(b, b, fore_sem, RING + name, x_mate))

    def pass_on(reach, c):
        rows = (lower, upper)[c]
        if reach < REACH or c == 0:
            b = block(place, z // 2 - reach + 1, rows)
            ups[reach, c] = go(send(b, b, ring_sem, reach * 2 + c, at(xl, y, (z + 2) % ZN)))
        if reach < REACH or c == 1:
            b = block(place, z // 2 + reach - 1, rows)
            downs[reach, c] = go(
                send(b, b, ring_sem, (REACH + 1 + reach) * 2 + c, at(xl, y, (z + ZN - 2) % ZN))
            )

    for c in range(2):
        pass_on(1, c)
    forward(0, z // 2)

    def names(reach):
        if reach == 0:
            return [(0, 0)]
        return [(reach, -reach)] + ([(REACH + reach, reach)] if reach < REACH else [])

    def tick(reach):
        for c in range(2):
            if (reach, c) in ups:
                ups[reach, c].wait_recv()
            if (reach, c) in downs:
                downs[reach, c].wait_recv()
            if reach < REACH:
                pass_on(reach + 1, c)
        if reach <= REACH:
            for name, away in names(reach):
                forward(name, z // 2 + away)
        for name, away in names(reach - 1):
            forward_beside(name, z // 2 + away)

    source = lax.broadcasted_iota(jnp.int32, (RUN, RUN), 0)
    target = lax.broadcasted_iota(jnp.int32, (RUN, RUN), 1)
    parity = (source // SPAN + z) % 2
    wanted = (source % SPAN) // COLS * (2 * COLS) + parity * COLS + source % COLS
    turns[...] = jnp.where(wanted == target, 1.0, 0.0).astype(BF16)

    loads[4].wait()
    loads[5].wait()
    loads[6].wait()
    for j in range(TILES):
        lanes = slice(j * 128, (j + 1) * 128)
        rate = rate_in[:, lanes] * (1.0 / LENGTH)
        rates[j] = rate
        keeps[j] = jnp.exp(-rate)
        weights[j] = mode_weight(rate, residue_in[:, lanes])
        for s in range(3):
            for t in range(TAPS):
                taps[j, s * TAPS + t : s * TAPS + t + 1, :] = taps_in[s, t : t + 1, lanes]
        line_rate[j : j + 1, :] = rates[j, pl.ds(z, 1), :]
        for s, stream in enumerate(streams):
            xs[s, j, :8, :] = jnp.zeros((8, 128), F32)
            xs[s, j, 8:, :] = stream[:, lanes].astype(F32)

    def features(j, first, last):
        tap = taps[j]
        prev = [
            [xs[s, j, pl.ds(8 + first - d, SEG, stride=STEPS), :] for d in (1, 2)] for s in range(3)
        ]
        products = []
        for i in range(first, last):
            out = []
            for s in range(3):
                f = [tap[s * TAPS + t : s * TAPS + t + 1] for t in range(TAPS)]
                x0 = xs[s, j, pl.ds(8 + i, SEG, stride=STEPS), :]
                x1, x2 = prev[s]
                out.append(rounded((f[0] * x0 + f[1] * x1) + f[2] * x2))
                prev[s] = [x0, x1]
            qconv[j, i] = out[0]
            p = rounded(out[1] * out[2])
            prod[j, i] = p
            products.append(p)
        return products

    segment = lax.broadcasted_iota(jnp.int32, (SEG, 128), 0)
    later = segment >= 1

    @pl.loop(0, TILES)
    def _(j):
        features(j, 0, STEPS)

    @pl.loop(0, TILES)
    def _(j):
        rate = rates[j]
        keep = keeps[j]
        decays = [jnp.broadcast_to(keep[n : n + 1], (SEG, 128)) for n in range(MODES)]
        states = [jnp.zeros((SEG, 128), F32) for _ in range(MODES)]
        for i in range(STEPS):
            p = prod[j, i]
            if i < TAPS - 1:
                p = jnp.where(later, p, 0.0)
            states = [d * st + p for d, st in zip(decays, states)]
        for n in range(MODES):
            a = rate[n : n + 1]
            total = states[n]
            for k in (1, 2, 4):
                moved = jnp.where(segment >= k, pltpu.roll(total, k, 0), 0.0)
                total = total + jnp.exp(a * (-float(STEPS * k))) * moved
            local[j, n] = jnp.where(later, pltpu.roll(total, 1, 0), 0.0)
            ends_own[j, n : n + 1, :] = total[SEG - 1 : SEG]

    halo.wait_recv()
    seen = jnp.where(ctx == 0, 0.0, 1.0).astype(F32)
    for s in range(3):
        for j in range(TILES):
            xs[s, j, 6:8, :] = halo_in[2 * s : 2 * s + 2, j * 128 : (j + 1) * 128] * seen

    def first_two(j):
        rate = rates[j]
        return prod[j, 0, 0:1] * jnp.exp(rate) + prod[j, 1, 0:1] * jnp.exp(2.0 * rate)

    @pl.loop(0, TILES)
    def _(j):
        features(j, 0, TAPS - 1)
        total = ends_own[j] + jnp.exp(rates[j] * -float(TOK)) * first_two(j)
        for n in range(MODES):
            ends[n, pl.ds(j, 1), :] = total[n : n + 1]

    def z_copy(i):
        o = HALF + (i // 2) * (1 - 2 * (i % 2))
        to = (z + o) % ZN
        return send(ends.at[to], z_in.at[z], z_sem, o, (row * ZN + to, ch))

    pl.semaphore_wait(line_sem, 2)

    @pl.loop(1, ZN)
    def _(o):
        z_copy(o).start()

    z_in[z] = ends[z]

    @pl.loop(0, TILES)
    def _(j):
        rate = rates[j]
        extra = first_two(j)
        for n in range(MODES):
            power = jnp.exp(rate[n : n + 1] * (segment * -STEPS).astype(F32))
            powers[j, n] = power
            local[j, n] = local[j, n] + jnp.where(later, power * extra[n : n + 1], 0.0)

    tick(1)

    @pl.loop(1, ZN)
    def _(o):
        z_copy(o).wait_recv()


    rate = line_rate[...]
    keep = jnp.exp(rate * -float(TOK))
    state = jnp.zeros((SEG, 128), F32)
    for zz in range(ZN):
        before[zz] = state
        state = keep * state + z_in[zz]
    totals[row] = state

    def row_copy(o):
        to = (row + o) % ROWS
        return send(totals.at[row], totals.at[row], row_sem, o, (to * ZN + z, ch))

    @pl.loop(1, ROWS)
    def _(o):
        row_copy(o).start()


    tick(2)

    @pl.loop(1, ROWS)
    def _(o):
        row_copy(o).wait_recv()


    keep_row = jnp.exp(rate * -float(TOK * ZN))
    state = jnp.zeros((SEG, 128), F32)
    for r in range(ROWS):
        state = jnp.where(r < row, keep_row * state + totals[r], state)
    for zz in range(ZN):
        carry_out[zz] = before[zz] + state
        state = keep * state

    def back_copy(i):
        o = HALF + (i // 2) * (1 - 2 * (i % 2))
        to = (z + o) % ZN
        return send(carry_out.at[to], carry_in.at[z], back_sem, o, (row * ZN + to, ch))

    @pl.loop(1, ZN)
    def _(o):
        back_copy(o).start()

    carry_in[z] = carry_out[z]

    tick(3)
    tick(4)

    @pl.loop(1, ZN)
    def _(o):
        back_copy(o).wait_recv()


    def gated(half):
        @pl.loop(half * (TILES // 2), (half + 1) * (TILES // 2))
        def _(j):
            keep = keeps[j]
            weight = weights[j]
            decays = [jnp.broadcast_to(keep[n : n + 1], (SEG, 128)) for n in range(MODES)]
            scales = [jnp.broadcast_to(weight[n : n + 1], (SEG, 128)) for n in range(MODES)]
            states = [
                local[j, n] + powers[j, n] * carry_in[n, pl.ds(j, 1), :] for n in range(MODES)
            ]
            for i in range(STEPS):
                p = prod[j, i]
                states = [d * st + p for d, st in zip(decays, states)]
                terms = [w * st for w, st in zip(scales, states)]
                while len(terms) > 1:
                    terms = [a + b for a, b in zip(terms[::2], terms[1::2])]
                gate[j, pl.ds(i, SEG, stride=STEPS), :] = qconv[j, i] * rounded(terms[0])

        for i in range(TILES // 2):
            lanes = slice(i * 128, (i + 1) * 128)
            pooled[half, 0, :, lanes] = gate[half * (TILES // 2) + i].astype(BF16)

    def pool(slot, to_slot, half, index, device):
        return go(send(pooled.at[half, slot], pooled.at[half, to_slot], pool_sem, index, device))

    gated(0)
    z_a = pool(0, 2, 0, 0, z_mate)
    gated(1)
    y_a = pool(0, 1, 1, 1, y_mate)
    z_b = pool(0, 2, 1, 2, z_mate)
    y_b = pool(0, 1, 0, 3, y_mate)

    tick(5)

    to_core, to_owner = {}, {}

    def product(first_b, last_b, half, side):
        depth = slice(half * (CHN // 2), (half + 1) * (CHN // 2))
        return lax.dot_general(
            pooled[half, first_b : last_b + 1].reshape((last_b + 1 - first_b) * TOK, CHN // 2),
            wg[2 * side : 2 * side + 2, :, :, depth].reshape(RUN, CHN // 2),
            (((1,), (1,)), ((), ())),
            preferred_element_type=F32,
        )

    def project(b, side, sums):
        for h in range(2):
            for c in range(2):
                quarter = sums[(h * 2 + c) * QTR : (h * 2 + c + 1) * QTR]
                part[b, c, h, side] = quarter
                part_out[b, c, h, side] = quarter.astype(BF16)

    def whole(first_b, last_b):
        for side in range(XN):
            sums = product(first_b, last_b, 0, side) + product(first_b, last_b, 1, side)
            for b in range(first_b, last_b + 1):
                project(b, side, sums[(b - first_b) * TOK : (b + 1 - first_b) * TOK])
        for b in range(first_b, last_b + 1):
            exchange(b)

    def exchange(b):
        to_core[b] = go(send(part_out.at[b, 1 - core], part_in.at[b], core_sem, b, mate))

    def add_core(b):
        to_core[b].wait_recv()
        for same, h in ((1, 1 - hi), (0, hi)):
            sums = part[b, core, h] + part_in[b, h].astype(F32)
            last_out[b, same] = sums.astype(BF16)
            if b == 0 and same == 0:
                last_in[0, 0] = sums.astype(BF16)
            else:
                to_owner[b, same] = go(
                    send(
                        last_out.at[b, same], last_in.at[b, same], last_sem, b * 2 + same,
                        at(xl, y_of[b], z_of[b], h * 2 + core),
                    )
                )

    def finish(bs):
        for i, b in enumerate(bs):
            for same in range(2):
                if (b, same) in to_owner:
                    to_owner[b, same].wait_recv()
            mixed = (last_in[b, 0].astype(F32) + last_in[b, 1].astype(F32)).astype(BF16)
            for side in range(XN):
                for k in range(2):
                    woven[side * 2 + k, :, i * SPAN : (i + 1) * SPAN] = mixed[side, :, k * SPAN : (k + 1) * SPAN]
        spread = lax.dot_general(
            woven[...].reshape(4 * QTR, RUN), turns[...], (((1,), (0,)), ((), ())),
            preferred_element_type=F32,
        ).astype(BF16)
        sender = y_of[bs[0]]
        role = (sender + sender // 2) % 2
        for side in range(XN):
            for k, at_y in enumerate((role, YN - 1 - role)):
                columns = pl.ds(pl.multiple_of(side * (YN * RUN) + at_y * RUN, RUN), RUN)
                out_ref[:, columns] = spread[(side * 2 + k) * QTR : (side * 2 + k + 1) * QTR]

    z_a.wait_recv()
    far_a = pool(2, 3, 0, 4, y_mate)
    y_a.wait_recv()
    far_b = pool(1, 3, 1, 5, z_mate)
    for copy in fore.values():
        copy.wait_recv()
    whole(0, 0)
    y_b.wait_recv()
    z_b.wait_recv()
    whole(1, 2)
    add_core(0)
    far_a.wait_recv()
    for side in range(XN):
        first[side] = product(3, 3, 0, side)
    add_core(1)
    add_core(2)
    far_b.wait_recv()
    for side in range(XN):
        project(3, side, first[side] + product(3, 3, 1, side))
    exchange(3)
    add_core(3)
    finish((0, 2))
    finish((1, 3))

    @pl.loop(1, ZN)
    def _(o):
        z_copy(o).wait_send()
        back_copy(o).wait_send()

    @pl.loop(1, ROWS)
    def _(o):
        row_copy(o).wait_send()

    for copy in started:
        copy.wait_send()


def shards(query_in, key_in, value_in, short_filter, decay_rate, residue, out_weight):
    def sems(count):
        return pltpu.SemaphoreType.DMA((2, count))

    return pl.pallas_call(
        kernel,
        out_shape=jax.ShapeDtypeStruct((QTR, 4096), BF16),
        in_specs=[pl.BlockSpec(memory_space=pl.ANY)] * 7,
        out_specs=pl.BlockSpec(memory_space=pltpu.VMEM),
        scratch_shapes=[
            pltpu.VMEM((TOK, CHN), BF16),
            pltpu.VMEM((TOK, CHN), BF16),
            pltpu.VMEM((TOK, CHN), BF16),
            pltpu.VMEM((3, TAPS, CHN), F32),
            pltpu.VMEM((MODES, CHN), F32),
            pltpu.VMEM((MODES, CHN), F32),
            pltpu.VMEM((COLS, CHN), BF16),
            pltpu.VMEM((TILES, 16, 128), F32),
            pltpu.VMEM((TILES, MODES, 128), F32),
            pltpu.VMEM((TILES, MODES, 128), F32),
            pltpu.VMEM((TILES, MODES, 128), F32),
            pltpu.VMEM((TILES, 128), F32),
            pltpu.VMEM((3, TILES, 8 + TOK, 128), F32),
            pltpu.VMEM((8, CHN), F32),
            pltpu.VMEM((8, CHN), F32),
            pltpu.VMEM((TILES, STEPS, SEG, 128), F32),
            pltpu.VMEM((TILES, STEPS, SEG, 128), F32),
            pltpu.VMEM((TILES, MODES, SEG, 128), F32),
            pltpu.VMEM((TILES, MODES, SEG, 128), F32),
            pltpu.VMEM((TILES, MODES, 128), F32),
            pltpu.VMEM((MODES, TILES, 128), F32),
            pltpu.VMEM((ZN, TILES, 128), F32),
            pltpu.VMEM((ZN, TILES, 128), F32),
            pltpu.VMEM((ROWS, TILES, 128), F32),
            pltpu.VMEM((ZN, TILES, 128), F32),
            pltpu.VMEM((MODES, TILES, 128), F32),
            pltpu.VMEM((TILES, TOK, 128), F32),
            pltpu.VMEM((2, 4, TOK, CHN // 2), BF16),
            pltpu.VMEM((2 * XN, RING, COLS, CHN), BF16),
            pltpu.VMEM((XN, TOK, RUN), F32),
            pltpu.VMEM((YN, 2, 2, XN, QTR, RUN), F32),
            pltpu.VMEM((YN, 2, 2, XN, QTR, RUN), BF16),
            pltpu.VMEM((YN, 2, XN, QTR, RUN), BF16),
            pltpu.VMEM((YN, 2, XN, QTR, RUN), BF16),
            pltpu.VMEM((YN, 2, XN, QTR, RUN), BF16),
            pltpu.VMEM((4, QTR, RUN), BF16),
            pltpu.VMEM((RUN, RUN), BF16),
            pltpu.SemaphoreType.DMA((7,)),
            pltpu.SemaphoreType.REGULAR,
            sems(1),
            sems(ZN),
            sems(ROWS),
            sems(ZN),
            sems(2 * (REACH + 1) * 2),
            sems(RING),
            sems(ZN),
            sems(6),
            sems(YN),
            sems(YN * 2),
        ],
        compiler_params=pltpu.CompilerParams(
            collective_id=0, has_side_effects=True, vmem_limit_bytes=56 * 1024 * 1024
        ),
        cost_estimate=pl.CostEstimate(
            flops=2 * 4 * TOK * CHN * CHN, bytes_accessed=4 * 1024 * 1024, transcendentals=0
        ),
    )(
        query_in, key_in, value_in, short_filter,
        jnp.transpose(decay_rate), jnp.transpose(residue), jnp.transpose(out_weight),
    )


def solution(mesh):
    return jax.shard_map(
        shards,
        mesh=mesh,
        in_specs=(
            P("ctx", "ch"),
            P("ctx", "ch"),
            P("ctx", "ch"),
            P(None, None, "ch"),
            P("ch", None),
            P("ch", None),
            P("ch", "ctx"),
        ),
        out_specs=P(("ctx", "ch"), None),
        check_vma=False,
    )
```
